32 devices in a mesh: dp: 8 (over z, y), tensor: 4 (over x, core).
Axes of the slice: x: 2, y: 2, z: 4, core: 2. Of those that a mesh axis runs over, the one named last changes fastest.
Arguments:
- tokens: bfloat16 [12288, 640], P('dp'), may hold values from -6 to 6
- attend_weight: bfloat16 [640, 1920], P(None, 'tensor'), may hold values from -0.25 to 0.25
- attend_bias: float32 [20, 64], P('tensor'), may hold values from -3 to 3
- mixing_weight: bfloat16 [640, 640], P('tensor'), may hold values from -2 to 2
- mixing_bias: float32 [640], replicated, may hold values from -2 to 2
- expand_weight: bfloat16 [640, 5120], P(None, 'tensor'), may hold values from -0.25 to 0.25
- expand_bias: float32 [5120], P('tensor'), may hold values from -3 to 3
- shrink_weight: bfloat16 [5120, 640], P('tensor'), may hold values from -0.078125 to 0.078125
- shrink_bias: float32 [640], replicated, may hold values from -2 to 2
- first_gain: float32 [640], replicated, may hold values from 0.1 to 1.9
- first_shift: float32 [640], replicated, may hold values from -2 to 2
- second_gain: float32 [640], replicated, may hold values from 0.1 to 1.9
- second_shift: float32 [640], replicated, may hold values from -2 to 2
- item_lengths: int32 [8, 9], P('dp'), may hold values from 16 to 1024, as said below
- visible: int32 [12288], P('dp'), may hold values 0 or 1
- cotangent: bfloat16 [12288, 640], P('dp'), may hold values from -6 to 6
Outputs:
- layer_output: bfloat16 [12288, 640], P('dp')
- input_grad: float32 [12288, 640], P('dp')
- attend_weight_grad: float32 [640, 1920], P(None, 'tensor')
- attend_bias_grad: float32 [20, 64], P('tensor')
- mixing_weight_grad: float32 [640, 640], P('tensor')
- mixing_bias_grad: float32 [640], replicated
- expand_weight_grad: float32 [640, 5120], P(None, 'tensor')
- expand_bias_grad: float32 [5120], P('tensor')
- shrink_weight_grad: float32 [5120, 640], P('tensor')
- shrink_bias_grad: float32 [640], replicated
- first_gain_grad: float32 [640], replicated
- first_shift_grad: float32 [640], replicated
- second_gain_grad: float32 [640], replicated
- second_shift_grad: float32 [640], replicated
The draws below stay inside these ranges and needn't reach their ends.
Inputs may be any that keep to these rules, and one draw needn't show every extreme that they name: `item_lengths`: each bucket's items are packed from its first row; its first item is a window of exactly 1024 nucleotides or a short item, all others are short items of at most 64; at least one bucket holds a window, so the lengths of a bucket sum to at most 1536.
All inputs are finite; a program needn't handle non-finite values. No bound on the sum of `visible` on one device may be relied on, other than what follows from the above.
Results may differ from the reference program's by a relative error of at most 0.018.
Values may be sent and summed in bfloat16 or wider, within the bound.
A program may use at most 192 MiB of HBM per device.

```python
import jax
import jax.numpy as jnp
from jax import lax

D = 640
HEADS = 20
HEAD_DIM = 32
FF = 5120
WINDOW = 1024
SHORT_MOST = 64
ITEMS = 9
TOK_DEV = 1536
TOKENS = 12288
N_DP = 8
N_TENSOR = 4


def draw_item_lengths(key, part):
    key = jax.random.fold_in(key, 3)
    first_key, second_key, third_key = jax.random.split(key, 3)
    brief_items = jax.random.randint(first_key, (N_DP, ITEMS), SHORT_MOST // 4, SHORT_MOST + 1)
    flagged = jax.random.randint(second_key, (N_DP,), 0, 2)
    chosen = jax.random.randint(third_key, (), 0, N_DP)
    flagged = jnp.where(jnp.arange(N_DP) == chosen, 1, flagged)
    leading = jnp.where(flagged == 1, WINDOW, brief_items[:, 0])
    return jnp.concatenate([leading[:, None], brief_items[:, 1:]], axis=1).astype(jnp.int32)


def touch_ends(drawn, own_key, smallest, high):
    spot = [jax.random.randint(jax.random.fold_in(own_key, axis), (), 0, length) for axis, length in enumerate(drawn.shape)]
    main_axis = drawn.shape.index(max(drawn.shape))
    neighbour = spot[:main_axis] + [(spot[main_axis] + 1) % drawn.shape[main_axis]] + spot[main_axis + 1:]
    return drawn.at[tuple(spot)].set(smallest).at[tuple(neighbour)].set(high)


def shard_levels(key, dims, pieces, low, top_value):
    def one(axis_at, blocks):
        heights = jax.random.uniform(jax.random.fold_in(jax.random.fold_in(key, 6), axis_at), (blocks,), jnp.float32, low / len(pieces), top_value / len(pieces))
        return jnp.repeat(jnp.exp(heights), dims[axis_at] // blocks).reshape((-1,) + (1,) * (len(dims) - axis_at - 1))

    factor_of = one(*pieces[0])
    for cut in pieces[1:]:
        factor_of = factor_of * one(*cut)
    return factor_of


def scatter_about(stream_key, shape, scale, bound, shards=(), kind=jnp.bfloat16):
    loudness = shard_levels(stream_key, shape, shards, -0.22, 0.18) if shards else 1.0
    array = jax.random.normal(stream_key, shape, jnp.float32) * scale * loudness
    return jnp.minimum(jnp.maximum(array, -bound), bound).astype(kind)


def setup_inputs(seed: int = 0) -> dict:
    arg_keys = jax.random.split(jax.random.key(seed), 17)
    tokens = scatter_about(arg_keys[0], (TOKENS, D), 1.0, 6.0, ((0, 8),))
    attend_weight = scatter_about(arg_keys[1], (D, 3 * D), D ** -0.5, 0.25, ((1, 4),))
    attend_bias = scatter_about(arg_keys[2], (HEADS, 2 * HEAD_DIM), 0.5, 3.0, ((0, 4),), jnp.float32)
    mixing_weight = scatter_about(arg_keys[3], (D, D), (max(D // 64, 1)) ** -0.5, 2.0, ((0, 4),))
    mixing_bias = scatter_about(arg_keys[4], (D,), 0.3, 2.0, (), jnp.float32)
    expand_weight = scatter_about(arg_keys[5], (D, FF), D ** -0.5, 0.25, ((1, 4),))
    expand_bias = scatter_about(arg_keys[6], (FF,), 0.5, 3.0, ((0, 4),), jnp.float32)
    shrink_weight = scatter_about(arg_keys[7], (FF, D), FF ** -0.5, 0.078125, ((0, 4),))
    shrink_bias = scatter_about(arg_keys[8], (D,), 0.3, 2.0, (), jnp.float32)
    first_gain = jnp.clip(1.0 + 0.18 * jax.random.normal(arg_keys[9], (D,), jnp.float32), 0.1, 1.9)
    first_shift = scatter_about(arg_keys[10], (D,), 0.3, 2.0, (), jnp.float32)
    second_gain = jnp.clip(1.0 + 0.18 * jax.random.normal(arg_keys[11], (D,), jnp.float32), 0.1, 1.9)
    second_shift = scatter_about(arg_keys[12], (D,), 0.3, 2.0, (), jnp.float32)
    item_lengths = draw_item_lengths(jax.random.fold_in(arg_keys[16], 71), 0)
    visible = touch_ends((jax.random.randint(arg_keys[14], (TOKENS,), 0, 8) < 7).astype(jnp.int32), jax.random.fold_in(arg_keys[14], 1), 0, 1)
    cotangent = scatter_about(arg_keys[15], (TOKENS, D), 1.0, 6.0, ((0, 8),))
    return dict(tokens=tokens, attend_weight=attend_weight, attend_bias=attend_bias, mixing_weight=mixing_weight, mixing_bias=mixing_bias, expand_weight=expand_weight, expand_bias=expand_bias, shrink_weight=shrink_weight, shrink_bias=shrink_bias, first_gain=first_gain, first_shift=first_shift, second_gain=second_gain, second_shift=second_shift, item_lengths=item_lengths, visible=visible, cotangent=cotangent)


@jax.custom_vjp
def low(v):
    return lax.optimization_barrier(v.astype(jnp.bfloat16)).astype(jnp.float32)

@jax.custom_vjp
def low_back(v):
    return v

def low_keep(v):
    return (low(v), None)

def low_pass(kept, grad):
    return (grad,)

def back_keep(v):
    return (v, None)

def back_low(kept, grad):
    return (low(grad),)
low.defvjp(low_keep, low_pass)
low_back.defvjp(back_keep, back_low)
epsilon = 1e-05
masked_score = -1e+30
highest = lax.Precision.HIGHEST

def layer_norm(values, gain, shift):
    center = values - lax.optimization_barrier(jnp.mean(values, axis=-1, keepdims=True))
    spread = lax.optimization_barrier(jnp.mean(center * center, axis=-1, keepdims=True))
    return center * lax.rsqrt(spread + epsilon) * gain + shift

def block_layer(weights, block):
    attend_weight, attend_bias, mixing_weight, mixing_bias, expand_weight, expand_bias, shrink_weight, shrink_bias, first_gain, first_shift, second_gain, second_shift = weights
    inputs, item_of, visible, valid = block
    height = inputs.shape[0]
    normed = low(layer_norm(inputs, first_gain, first_shift))
    joined = jnp.dot(normed, attend_weight, precision=highest).reshape(height, HEADS, 3, HEAD_DIM)
    query = low(low_back(joined[:, :, 0] + attend_bias[:, :HEAD_DIM]))
    keys = low(low_back(joined[:, :, 1]))
    values = low(low_back(joined[:, :, 2] + attend_bias[:, HEAD_DIM:]))
    place = jnp.arange(height, dtype=jnp.int32)
    allowed = (item_of[:, None] == item_of[None, :]) & ((visible[None, :] == 1) | (place[:, None] == place[None, :]))
    scores = jnp.einsum('qhd,khd->hqk', query, keys, precision=highest) * HEAD_DIM ** (-0.5)
    scores = jnp.where(allowed[None], low_back(scores), masked_score)
    row_max = lax.optimization_barrier(jnp.max(scores, axis=-1, keepdims=True))
    powers = jnp.exp(scores - row_max)
    probs = low(powers / lax.optimization_barrier(jnp.sum(powers, axis=-1, keepdims=True)))
    context = jnp.einsum('hqk,khd->qhd', probs, values, precision=highest).reshape(height, D)
    context = low(low_back(context))
    parts = jnp.einsum('tnc,nce->nte', context.reshape(height, N_TENSOR, D // N_TENSOR), mixing_weight.reshape(N_TENSOR, D // N_TENSOR, D), precision=highest)
    attn_sum = lax.optimization_barrier(jnp.sum(low(parts), axis=0))
    middle = inputs + low_back(attn_sum + mixing_bias) * valid[:, None]
    ffn_in = low(layer_norm(middle, second_gain, second_shift))
    hidden = low_back(jnp.dot(ffn_in, expand_weight, precision=highest) + expand_bias)
    act = low(jax.nn.gelu(hidden, approximate=False))
    parts = jnp.einsum('tnc,nce->nte', act.reshape(height, N_TENSOR, FF // N_TENSOR), shrink_weight.reshape(N_TENSOR, FF // N_TENSOR, D), precision=highest)
    ffn_sum = lax.optimization_barrier(jnp.sum(low(parts), axis=0))
    return middle + low_back(ffn_sum + shrink_bias) * valid[:, None]

def reference(tokens, attend_weight, attend_bias, mixing_weight, mixing_bias, expand_weight, expand_bias, shrink_weight, shrink_bias, first_gain, first_shift, second_gain, second_shift, item_lengths, visible, cotangent):
    ends = jnp.cumsum(item_lengths, axis=1).astype(jnp.int32)
    place = jnp.arange(TOK_DEV, dtype=jnp.int32)
    item_of = lax.optimization_barrier(jnp.sum((place[None, :, None] >= ends[:, None, :]).astype(jnp.int32), axis=2)).astype(jnp.int32)
    valid = (place[None, :] < ends[:, -1:]).astype(jnp.float32)
    inputs = tokens.astype(jnp.float32).reshape(N_DP, TOK_DEV, D)
    weights = (attend_weight.astype(jnp.float32), attend_bias, mixing_weight.astype(jnp.float32), mixing_bias, expand_weight.astype(jnp.float32), expand_bias, shrink_weight.astype(jnp.float32), shrink_bias, first_gain, first_shift, second_gain, second_shift)
    visible_rows = visible.reshape(N_DP, TOK_DEV)

    def forward(weight_set, activations):

        def one_block(block):
            return block_layer(weight_set, block)
        return lax.map(jax.checkpoint(one_block), (activations, item_of, visible_rows, valid))
    output, pullback = jax.vjp(forward, weights, inputs)
    weight_grads, input_grad = pullback(cotangent.astype(jnp.float32).reshape(N_DP, TOK_DEV, D))
    factor = N_DP / jnp.sum(item_lengths).astype(jnp.float32)
    scaled = [grad * factor for grad in weight_grads]
    return (output.reshape(TOKENS, D).astype(jnp.bfloat16), input_grad.reshape(TOKENS, D), scaled[0], scaled[1], scaled[2], scaled[3], scaled[4], scaled[5], scaled[6], scaled[7], scaled[8], scaled[9], scaled[10], scaled[11])
```

```python
import functools

import jax
import jax.numpy as jnp
from jax import lax
from jax.experimental import pallas as pl
from jax.experimental.pallas import tpu as pltpu
from jax.sharding import PartitionSpec as P

HEAD_DIM = 32
LANES = 256
SPAN = 512
HALF = SPAN // 2
WINDOW = 1024
BAND = 64
EPS = 1e-05
LOG2E = 1.4426950408889634
MASKED = -1e30
MESH = pl.DeviceIdType.MESH
f32 = jnp.float32
bf16 = jnp.bfloat16
VMEM = pl.BlockSpec(memory_space=pltpu.VMEM)
SMEM = pl.BlockSpec(memory_space=pltpu.SMEM)


def dot(left, right, left_dim=1, right_dim=0):
    return lax.dot_general(
        left, right, (((left_dim,), (right_dim,)), ((), ())), preferred_element_type=f32
    )


def norm_parts(values):
    center = values - jnp.mean(values, axis=-1, keepdims=True)
    spread = jnp.mean(center * center, axis=-1, keepdims=True)
    rate = lax.rsqrt(spread + EPS)
    return center * rate, rate


def norm_back(grad, gain, unit, rate):
    scaled = grad * gain
    first = jnp.mean(scaled, axis=-1, keepdims=True)
    second = jnp.mean(scaled * unit, axis=-1, keepdims=True)
    return rate * (scaled - first - unit * second)


def neighbours():
    place = lax.axis_index("tensor")
    core = place % 2
    chip = place // 2
    return core, chip * 2 + (1 - core), (1 - chip) * 2 + core


def greet(sibling, across):
    barrier = pltpu.get_barrier_semaphore()
    for other in (sibling, across):
        pl.semaphore_signal(barrier, inc=1, device_id={"tensor": other}, device_id_type=MESH)
    pl.semaphore_wait(barrier, 2)


def send(source, target, sems, slot, other):
    return pltpu.make_async_remote_copy(
        src_ref=source,
        dst_ref=target,
        send_sem=sems.at[0, slot],
        recv_sem=sems.at[1, slot],
        device_id={"tensor": other},
        device_id_type=MESH,
    )


def rows(start, count):
    return pl.ds(pl.multiple_of(start, count), count)


def item_ends(lengths_ref):
    ends = []
    total = 0
    for slot in range(lengths_ref.shape[1]):
        total = total + lengths_ref[0, slot]
        ends.append(total)
    return ends


def item_at(place, ends):
    item = jnp.zeros(place.shape, jnp.int32)
    for end in ends:
        item = item + (place >= end).astype(jnp.int32)
    return item


def mask_tile(ends, visible, row_start, count, key_start, keys):
    row = row_start + lax.broadcasted_iota(jnp.int32, (count, 1), 0)
    key = key_start + lax.broadcasted_iota(jnp.int32, (1, keys), 1)
    allowed = (item_at(row, ends) == item_at(key, ends)) & ((visible == 1) | (row == key))
    return jnp.where(allowed, 0.0, MASKED).astype(f32)


def head_lanes(head, kind):
    lane = lax.broadcasted_iota(jnp.int32, (1, LANES), 1)
    return ((lane >= head * HEAD_DIM) & (lane < (head + 1) * HEAD_DIM)).astype(f32).astype(kind)


def spread_columns(heads):
    source = lax.broadcasted_iota(jnp.int32, (heads * 3 * HEAD_DIM, 3 * LANES), 0)
    target = lax.broadcasted_iota(jnp.int32, (heads * 3 * HEAD_DIM, 3 * LANES), 1)
    part = target // LANES
    inside = target % LANES
    wanted = (inside // HEAD_DIM) * (3 * HEAD_DIM) + part * HEAD_DIM + inside % HEAD_DIM
    return ((source == wanted) & (inside < heads * HEAD_DIM)).astype(f32).astype(bf16)


def valid_rows(ends, start, count):
    row = start + lax.broadcasted_iota(jnp.int32, (count, 1), 0)
    return (row < ends[-1]).astype(f32)


SCALE = HEAD_DIM ** (-0.5)


def attend_kernel(
    heads,
    tokens,
    attend_weight,
    attend_bias,
    mixing_weight,
    mixing_bias,
    first_gain,
    first_shift,
    second_gain,
    second_shift,
    lengths,
    visible,
    normed,
    joined,
    wide_weight,
    context,
    log_totals,
    middle,
    ffn_in,
    wide_mixing,
    masks,
    part,
    from_core,
    chip_sum,
    from_chip,
    core_sems,
    chip_sems,
    share_sems,
):
    core, sibling, across = neighbours()
    height = tokens.shape[0]
    blocks = height // SPAN
    ends = item_ends(lengths)
    width = heads * HEAD_DIM
    greet(sibling, across)

    wide_weight[...] = dot(attend_weight[...], spread_columns(heads)).astype(bf16)
    wide_mixing[...] = jnp.zeros_like(wide_mixing)
    wide_mixing[0:width, :] = mixing_weight[...]

    def project(step, carry):
        where = rows(step * HALF, HALF)
        unit, _ = norm_parts(tokens[where, :].astype(f32))
        fresh = (unit * first_gain[...] + first_shift[...]).astype(bf16)
        normed[where, :] = fresh
        joined[where, :] = (dot(fresh, wide_weight[...]) + attend_bias[...]).astype(bf16)
        return carry

    lax.fori_loop(0, height // HALF, project, 0)

    def attend(row_start, count, key_start, keys):
        query = joined[pl.ds(row_start, count), 0:LANES]
        key_rows = pl.ds(key_start, keys)
        key = joined[key_rows, LANES : 2 * LANES]
        value = joined[key_rows, 2 * LANES : 3 * LANES]
        masks[0:count, 0:keys] = mask_tile(
            ends, visible[:, key_rows], row_start, count, key_start, keys
        )
        lane = lax.broadcasted_iota(jnp.int32, (1, 128), 1)
        mixed = jnp.zeros((count, LANES), f32)
        stats = jnp.zeros((count, 128), f32)
        for head in range(heads):
            scores = dot(query * head_lanes(head, bf16), key, 1, 1)
            scores = scores * (SCALE * LOG2E) + masks[0:count, 0:keys]
            top = jnp.max(scores, axis=-1, keepdims=True)
            powers = jnp.exp2(scores - top)
            total = jnp.sum(powers, axis=-1, keepdims=True)
            mine = dot(powers.astype(bf16), value) / total
            mixed = mixed + mine * head_lanes(head, f32)
            stats = jnp.where(lane == head, top + jnp.log2(total), stats)
        context[pl.ds(row_start, count), :] = mixed.astype(bf16)
        log_totals[pl.ds(row_start, count), :] = stats

    def mix(block):
        where = rows(block * SPAN, SPAN)
        part[where, :] = dot(context[where, :], wide_mixing[...]).astype(bf16)
        theirs = rows(block * SPAN + (1 - core) * HALF, HALF)
        to_core = send(part.at[theirs, :], from_core.at[block], core_sems, block, sibling)
        to_core.start()
        return to_core

    def cross(block, to_core):
        to_core.wait()
        ours = rows(block * SPAN + core * HALF, HALF)
        chip_sum[block] = (part[ours, :].astype(f32) + from_core[block].astype(f32)).astype(bf16)
        to_chip = send(chip_sum.at[block], from_chip.at[block], chip_sems, block, across)
        to_chip.start()
        return to_chip

    def finish(block, to_chip):
        to_chip.wait()
        start = block * SPAN + core * HALF
        ours = rows(start, HALF)
        total = chip_sum[block].astype(f32) + from_chip[block].astype(f32)
        center = tokens[ours, :].astype(f32) + (total + mixing_bias[...]) * valid_rows(
            ends, start, HALF
        )
        middle[block * HALF : (block + 1) * HALF, :] = center
        unit, _ = norm_parts(center)
        ffn_in[ours, :] = (unit * second_gain[...] + second_shift[...]).astype(bf16)
        share = send(ffn_in.at[ours, :], ffn_in.at[ours, :], share_sems, block, sibling)
        share.start()
        return share

    def short_step(step, carry):
        start = pl.multiple_of(WINDOW + step * 128, 128)
        first = pl.multiple_of(lax.min(start - BAND, height - 256), 64)
        attend_short(start, first)
        return carry

    def attend_short(start, first):
        attend(start, 128, first, 256)

    def dense_step(step, carry):
        attend(pl.multiple_of(step * HALF, HALF), HALF, 0, WINDOW)
        return carry

    del short_step
    for step in range((height - WINDOW) // 128):
        start = WINDOW + step * 128
        attend(start, 128, min(start - 128, height - 384), 384)
    core_copies = {2: mix(2)}
    chip_copies = {}
    lax.fori_loop(0, 1, dense_step, 0)
    chip_copies[2] = cross(2, core_copies[2])
    lax.fori_loop(1, 2, dense_step, 0)
    core_copies[0] = mix(0)
    lax.fori_loop(2, 3, dense_step, 0)
    chip_copies[0] = cross(0, core_copies[0])
    lax.fori_loop(3, 4, dense_step, 0)
    core_copies[1] = mix(1)
    chip_copies[1] = cross(1, core_copies[1])
    shares = [finish(block, chip_copies[block]) for block in (2, 0, 1)]
    for share in shares:
        share.wait()


def ffn_kernel(
    ffn_in,
    cotangent,
    middle,
    expand_weight,
    expand_bias,
    shrink_weight,
    shrink_bias,
    second_gain,
    lengths,
    layer_output,
    expand_grad,
    shrink_grad,
    expand_bias_grad,
    shrink_bias_grad,
    middle_back,
    attn_back,
    gain_grad,
    shift_grad,
    act,
    hidden_back,
    ffn_back,
    part,
    part_out,
    from_core,
    from_core_out,
    chip_sum,
    chip_sum_out,
    from_chip,
    from_chip_out,
    core_sems,
    chip_sems,
    share_sems,
    core_out_sems,
    chip_out_sems,
    share_out_sems,
):
    core, sibling, across = neighbours()
    height = ffn_in.shape[0]
    hidden_units = expand_weight.shape[1]
    blocks = height // SPAN
    ends = item_ends(lengths)
    greet(sibling, across)
    expand_bias_grad[...] = jnp.zeros_like(expand_bias_grad)
    shrink_bias_grad[...] = jnp.zeros_like(shrink_bias_grad)
    gain_grad[...] = jnp.zeros_like(gain_grad)
    shift_grad[...] = jnp.zeros_like(shift_grad)
    chunk = 256

    def work(block, step):
        start = block * SPAN + step * chunk
        where = rows(start, chunk)
        back = (cotangent[where, :].astype(f32) * valid_rows(ends, start, chunk)).astype(bf16)
        ffn_back[where, :] = back
        shrink_bias_grad[...] += jnp.sum(back.astype(f32), axis=0, keepdims=True)
        hidden = dot(ffn_in[where, :], expand_weight[...]) + expand_bias[...]
        smooth = 0.5 + 0.5 * lax.erf(hidden * (0.5**0.5))
        act[where, :] = (hidden * smooth).astype(bf16)
        slope = smooth + hidden * (0.3989422804014327 * jnp.exp2(hidden * hidden * (-0.5 * LOG2E)))
        fresh = (slope * dot(back, shrink_weight[...], 1, 1)).astype(bf16)
        hidden_back[where, :] = fresh
        expand_bias_grad[...] += jnp.sum(fresh.astype(f32), axis=0, keepdims=True)
        part[where, :] = dot(fresh, expand_weight[...], 1, 1).astype(bf16)

    def work_out(block, step):
        where = rows(block * SPAN + step * chunk, chunk)
        part_out[where, :] = dot(act[where, :], shrink_weight[...]).astype(bf16)

    def to_core(block, source, target, sems):
        theirs = rows(block * SPAN + (1 - core) * HALF, HALF)
        copy = send(source.at[theirs, :], target.at[block], sems, block, sibling)
        copy.start()
        return copy

    def cross(block, copy, source, arrived, total, target, sems):
        copy.wait()
        ours = rows(block * SPAN + core * HALF, HALF)
        total[block] = (source[ours, :].astype(f32) + arrived[block].astype(f32)).astype(bf16)
        copy = send(total.at[block], target.at[block], sems, block, across)
        copy.start()
        return copy

    def finish(block, copy):
        copy.wait()
        start = block * SPAN + core * HALF
        ours = rows(start, HALF)
        grad = chip_sum[block].astype(f32) + from_chip[block].astype(f32)
        unit, rate = norm_parts(middle[block * HALF : (block + 1) * HALF, :])
        gain_grad[...] += jnp.sum(grad * unit, axis=0, keepdims=True)
        shift_grad[...] += jnp.sum(grad, axis=0, keepdims=True)
        full = cotangent[ours, :].astype(f32) + norm_back(grad, second_gain[...], unit, rate)
        middle_back[block * HALF : (block + 1) * HALF, :] = full
        attn_back[ours, :] = (full * valid_rows(ends, start, HALF)).astype(bf16)
        share = send(attn_back.at[ours, :], attn_back.at[ours, :], share_sems, block, sibling)
        share.start()
        return share

    def finish_out(block, copy):
        copy.wait()
        start = block * SPAN + core * HALF
        ours = rows(start, HALF)
        total = chip_sum_out[block].astype(f32) + from_chip_out[block].astype(f32)
        layer_output[ours, :] = (
            middle[block * HALF : (block + 1) * HALF, :]
            + (total + shrink_bias[...]) * valid_rows(ends, start, HALF)
        ).astype(bf16)
        share = send(
            layer_output.at[ours, :], layer_output.at[ours, :], share_out_sems, block, sibling
        )
        share.start()
        return share

    order = (2, 0, 1)
    copies = {}
    outs = {}
    previous = None
    for block in order:
        for step in range(SPAN // chunk):
            work(block, step)
            if step == 0 and previous is not None:
                copies[previous] = cross(
                    previous, copies[previous], part, from_core, chip_sum, from_chip, chip_sems
                )
        copies[block] = to_core(block, part, from_core, core_sems)
        previous = block
    for step in range(SPAN // chunk):
        work_out(order[0], step)
    copies[previous] = cross(
        previous, copies[previous], part, from_core, chip_sum, from_chip, chip_sems
    )
    outs[order[0]] = to_core(order[0], part_out, from_core_out, core_out_sems)
    for block in order[1:]:
        for step in range(SPAN // chunk):
            work_out(block, step)
        outs[block] = to_core(block, part_out, from_core_out, core_out_sems)
    for block in order:
        outs[block] = cross(
            block,
            outs[block],
            part_out,
            from_core_out,
            chip_sum_out,
            from_chip_out,
            chip_out_sems,
        )
    shrink_grad[...] = dot(act[...], ffn_back[...], 0, 0).astype(bf16)
    shares = [finish(order[0], copies[order[0]])]
    expand_grad[...] = dot(ffn_in[...], hidden_back[...], 0, 0).astype(bf16)
    for block in order[1:]:
        shares.append(finish(block, copies[block]))
    for block in order:
        shares.append(finish_out(block, outs[block]))
    for share in shares:
        share.wait()


def back_kernel(
    heads,
    tokens,
    normed,
    joined,
    wide_weight,
    context,
    log_totals,
    attn_back,
    middle_back,
    mixing_weight,
    first_gain,
    lengths,
    visible,
    input_grad,
    attend_grad,
    mixing_grad,
    attend_bias_grad,
    mixing_bias_grad,
    gain_grad,
    shift_grad,
    wide_mixing,
    context_back,
    joined_back,
    key_grad,
    value_grad,
    masks,
    score_stack,
    prob_stack,
    part,
    from_core,
    chip_sum,
    from_chip,
    core_sems,
    chip_sems,
    share_sems,
):
    core, sibling, across = neighbours()
    height = tokens.shape[0]
    ends = item_ends(lengths)
    width = heads * HEAD_DIM
    greet(sibling, across)
    wide_mixing[...] = jnp.zeros_like(wide_mixing)
    wide_mixing[0:width, :] = mixing_weight[...]
    gain_grad[...] = jnp.zeros_like(gain_grad)
    shift_grad[...] = jnp.zeros_like(shift_grad)
    key_grad[...] = jnp.zeros_like(key_grad)
    value_grad[...] = jnp.zeros_like(value_grad)
    context_back[...] = dot(attn_back[...], wide_mixing[...], 1, 1).astype(bf16)

    def attend(row_start, count, key_start, keys):
        where = pl.ds(row_start, count)
        key_rows = pl.ds(key_start, keys)
        query = joined[where, 0:LANES]
        key = joined[key_rows, LANES : 2 * LANES]
        value = joined[key_rows, 2 * LANES : 3 * LANES]
        back = context_back[where, :]
        overlap = back.astype(f32) * context[where, :].astype(f32)
        masks[0:count, 0:keys] = mask_tile(
            ends, visible[:, key_rows], row_start, count, key_start, keys
        )
        query_grad = jnp.zeros((count, LANES), f32)
        for head in range(heads):
            mine = head_lanes(head, bf16)
            scores = dot(query * mine, key, 1, 1)
            scores = scores * (SCALE * LOG2E) + masks[0:count, 0:keys]
            probs = jnp.exp2(scores - log_totals[where, head : head + 1])
            delta = jnp.sum(overlap * head_lanes(head, f32), axis=-1, keepdims=True)
            change = probs * (dot(back * mine, value, 1, 1) - delta)
            low_change = change.astype(bf16)
            prob_stack[head * count : (head + 1) * count, 0:keys] = probs.astype(bf16)
            score_stack[head * count : (head + 1) * count, 0:keys] = low_change
            query_grad = query_grad + dot(low_change, key) * head_lanes(head, f32)
        joined_back[where, 0:LANES] = (query_grad * SCALE).astype(bf16)
        many_query = jnp.concatenate([query * head_lanes(h, bf16) for h in range(heads)], axis=0)
        many_back = jnp.concatenate([back * head_lanes(h, bf16) for h in range(heads)], axis=0)
        key_grad[key_rows, :] += dot(score_stack[0 : heads * count, 0:keys], many_query, 0, 0)
        value_grad[key_rows, :] += dot(prob_stack[0 : heads * count, 0:keys], many_back, 0, 0)

    def dense_step(step, carry):
        attend(pl.multiple_of(step * HALF, HALF), HALF, 0, WINDOW)
        return carry

    def project(block):
        where = rows(block * SPAN, SPAN)
        joined_back[where, LANES : 2 * LANES] = (key_grad[where, :] * SCALE).astype(bf16)
        joined_back[where, 2 * LANES : 3 * LANES] = value_grad[where, :].astype(bf16)
        part[where, :] = dot(joined_back[where, :], wide_weight[...], 1, 1).astype(bf16)
        theirs = rows(block * SPAN + (1 - core) * HALF, HALF)
        copy = send(part.at[theirs, :], from_core.at[block], core_sems, block, sibling)
        copy.start()
        return copy

    def cross(block, copy):
        copy.wait()
        ours = rows(block * SPAN + core * HALF, HALF)
        chip_sum[block] = (part[ours, :].astype(f32) + from_core[block].astype(f32)).astype(bf16)
        copy = send(chip_sum.at[block], from_chip.at[block], chip_sems, block, across)
        copy.start()
        return copy

    def finish(block, copy):
        copy.wait()
        ours = rows(block * SPAN + core * HALF, HALF)
        grad = chip_sum[block].astype(f32) + from_chip[block].astype(f32)
        unit, rate = norm_parts(tokens[ours, :].astype(f32))
        gain_grad[...] += jnp.sum(grad * unit, axis=0, keepdims=True)
        shift_grad[...] += jnp.sum(grad, axis=0, keepdims=True)
        input_grad[ours, :] = middle_back[block * HALF : (block + 1) * HALF, :] + norm_back(
            grad, first_gain[...], unit, rate
        )
        share = send(input_grad.at[ours, :], input_grad.at[ours, :], share_sems, block, sibling)
        share.start()
        return share

    for step in range((height - WINDOW) // 128):
        start = WINDOW + step * 128
        attend(start, 128, min(start - 128, height - 384), 384)
    copies = {}
    lax.fori_loop(0, WINDOW // HALF, dense_step, 0)
    for block in (2, 0, 1):
        copies[block] = project(block)
    for block in (2, 0, 1):
        copies[block] = cross(block, copies[block])
    shares = [finish(2, copies[2])]
    mixing_grad[...] = dot(context[...], attn_back[...], 0, 0)[0:width, :].astype(bf16)
    mixing_bias_grad[...] = jnp.sum(attn_back[...].astype(f32), axis=0, keepdims=True)
    wide = dot(normed[...], joined_back[...], 0, 0).astype(bf16)
    attend_grad[...] = dot(wide, spread_columns(heads), 1, 1).astype(bf16)
    attend_bias_grad[...] = jnp.sum(joined_back[...].astype(f32), axis=0, keepdims=True)
    shares += [finish(block, copies[block]) for block in (0, 1)]
    for share in shares:
        share.wait()


def shape(*dims, kind=bf16):
    return jax.ShapeDtypeStruct(dims, kind)


def params(number):
    return pltpu.CompilerParams(
        collective_id=number, has_side_effects=True, vmem_limit_bytes=60 * 2**20
    )


def sems(blocks):
    return pltpu.SemaphoreType.DMA((2, blocks))


def per_device(
    tokens,
    attend_weight,
    attend_bias,
    mixing_weight,
    mixing_bias,
    expand_weight,
    expand_bias,
    shrink_weight,
    shrink_bias,
    first_gain,
    first_shift,
    second_gain,
    second_shift,
    item_lengths,
    visible,
    cotangent,
):
    height, depth = tokens.shape
    heads = attend_bias.shape[0]
    units = expand_weight.shape[1]
    width = heads * HEAD_DIM
    blocks = height // SPAN
    own = height // 2
    visible = visible[None, :]
    row = lambda vector: vector[None, :]
    pad = ((0, 0), (0, LANES - width))
    bias = jnp.concatenate(
        [
            jnp.pad(attend_bias[:, :HEAD_DIM].reshape(1, width), pad),
            jnp.zeros((1, LANES), f32),
            jnp.pad(attend_bias[:, HEAD_DIM:].reshape(1, width), pad),
        ],
        axis=1,
    )
    count = lax.psum(jnp.sum(item_lengths), "dp")

    normed, joined, wide_weight, context, log_totals, middle, ffn_in = pl.pallas_call(
        functools.partial(attend_kernel, heads),
        out_shape=(
            shape(height, depth),
            shape(height, 3 * LANES),
            shape(depth, 3 * LANES),
            shape(height, LANES),
            shape(height, 128, kind=f32),
            shape(own, depth, kind=f32),
            shape(height, depth),
        ),
        in_specs=[VMEM] * 9 + [SMEM, VMEM],
        out_specs=(VMEM,) * 7,
        scratch_shapes=[
            pltpu.VMEM((LANES, depth), bf16),
            pltpu.VMEM((HALF, WINDOW), f32),
            pltpu.VMEM((height, depth), bf16),
            pltpu.VMEM((blocks, HALF, depth), bf16),
            pltpu.VMEM((blocks, HALF, depth), bf16),
            pltpu.VMEM((blocks, HALF, depth), bf16),
            sems(blocks),
            sems(blocks),
            sems(blocks),
        ],
        compiler_params=params(0),
        name="attend",
    )(
        tokens,
        attend_weight,
        bias,
        mixing_weight,
        row(mixing_bias),
        row(first_gain),
        row(first_shift),
        row(second_gain),
        row(second_shift),
        item_lengths,
        visible,
    )

    (
        layer_output,
        expand_grad,
        shrink_grad,
        expand_bias_grad,
        shrink_bias_grad,
        middle_back,
        attn_back,
        second_gain_grad,
        second_shift_grad,
    ) = pl.pallas_call(
        ffn_kernel,
        out_shape=(
            shape(height, depth),
            shape(depth, units),
            shape(units, depth),
            shape(1, units, kind=f32),
            shape(1, depth, kind=f32),
            shape(own, depth, kind=f32),
            shape(height, depth),
            shape(1, depth, kind=f32),
            shape(1, depth, kind=f32),
        ),
        in_specs=[VMEM] * 8 + [SMEM],
        out_specs=(VMEM,) * 9,
        scratch_shapes=[
            pltpu.VMEM((height, units), bf16),
            pltpu.VMEM((height, units), bf16),
            pltpu.VMEM((height, depth), bf16),
            pltpu.VMEM((height, depth), bf16),
            pltpu.VMEM((height, depth), bf16),
        ]
        + [pltpu.VMEM((blocks, HALF, depth), bf16)] * 6
        + [sems(blocks)] * 6,
        compiler_params=params(1),
        name="feed",
    )(
        ffn_in,
        cotangent,
        middle,
        expand_weight,
        row(expand_bias),
        shrink_weight,
        row(shrink_bias),
        row(second_gain),
        item_lengths,
    )

    expand_sum, shrink_sum = lax.psum((expand_grad, shrink_grad), "dp")

    (
        input_grad,
        attend_grad,
        mixing_grad,
        attend_bias_grad,
        mixing_bias_grad,
        first_gain_grad,
        first_shift_grad,
    ) = pl.pallas_call(
        functools.partial(back_kernel, heads),
        out_shape=(
            shape(height, depth, kind=f32),
            shape(depth, 3 * width),
            shape(width, depth),
            shape(1, 3 * LANES, kind=f32),
            shape(1, depth, kind=f32),
            shape(1, depth, kind=f32),
            shape(1, depth, kind=f32),
        ),
        in_specs=[VMEM] * 10 + [SMEM, VMEM],
        out_specs=(VMEM,) * 7,
        scratch_shapes=[
            pltpu.VMEM((LANES, depth), bf16),
            pltpu.VMEM((height, LANES), bf16),
            pltpu.VMEM((height, 3 * LANES), bf16),
            pltpu.VMEM((height, LANES), f32),
            pltpu.VMEM((height, LANES), f32),
            pltpu.VMEM((HALF, WINDOW), f32),
            pltpu.VMEM((heads * HALF, WINDOW), bf16),
            pltpu.VMEM((heads * HALF, WINDOW), bf16),
            pltpu.VMEM((height, depth), bf16),
            pltpu.VMEM((blocks, HALF, depth), bf16),
            pltpu.VMEM((blocks, HALF, depth), bf16),
            pltpu.VMEM((blocks, HALF, depth), bf16),
        ]
        + [sems(blocks)] * 3,
        compiler_params=params(2),
        name="back",
    )(
        tokens,
        normed,
        joined,
        wide_weight,
        context,
        log_totals,
        attn_back,
        middle_back,
        mixing_weight,
        row(first_gain),
        item_lengths,
        visible,
    )

    halved = jnp.concatenate(
        [second_gain_grad, second_shift_grad, first_gain_grad, first_shift_grad], axis=0
    )
    halved = lax.psum(halved * 0.5, ("dp", "tensor"))
    attend_bias_local = jnp.concatenate(
        [
            attend_bias_grad[:, :width].reshape(heads, HEAD_DIM),
            attend_bias_grad[:, 2 * LANES : 2 * LANES + width].reshape(heads, HEAD_DIM),
        ],
        axis=1,
    )
    merged = lax.psum(
        (attend_bias_local, mixing_bias_grad, expand_bias_grad, shrink_bias_grad), "dp"
    )
    attend_sum, mixing_sum = lax.psum((attend_grad, mixing_grad), "dp")
    factor = lax.axis_size("dp") / count.astype(f32)
    return (
        layer_output,
        input_grad,
        attend_sum.astype(f32) * factor,
        merged[0] * factor,
        mixing_sum.astype(f32) * factor,
        merged[1][0] * factor,
        expand_sum.astype(f32) * factor,
        merged[2][0] * factor,
        shrink_sum.astype(f32) * factor,
        merged[3][0] * factor,
        halved[2] * factor,
        halved[3] * factor,
        halved[0] * factor,
        halved[1] * factor,
    )


def solution(mesh):
    placed = (
        P("dp", None),
        P(None, "tensor"),
        P("tensor", None),
        P("tensor", None),
        P(),
        P(None, "tensor"),
        P("tensor"),
        P("tensor", None),
        P(),
        P(),
        P(),
        P(),
        P(),
        P("dp", None),
        P("dp"),
        P("dp", None),
    )
    return jax.shard_map(
        per_device,
        mesh=mesh,
        in_specs=placed,
        out_specs=(
            P("dp", None),
            P("dp", None),
            P(None, "tensor"),
            P("tensor", None),
            P("tensor", None),
            P(),
            P(None, "tensor"),
            P("tensor"),
            P("tensor", None),
            P(),
            P(),
            P(),
            P(),
            P(),
        ),
        check_vma=False,
    )
```

```python
import functools

import jax
import jax.numpy as jnp
from jax import lax
from jax.experimental import pallas as pl
from jax.experimental.pallas import tpu as pltpu
from jax.sharding import PartitionSpec as P

HEAD_DIM = 32
LANES = 256
SPAN = 512
HALF = SPAN // 2
WINDOW = 1024
EPS = 1e-05
LOG2E = 1.4426950408889634
MASKED = -1e30
MESH = pl.DeviceIdType.MESH
f32 = jnp.float32
bf16 = jnp.bfloat16
VMEM = pl.BlockSpec(memory_space=pltpu.VMEM)
ANY = pl.BlockSpec(memory_space=pl.ANY)
SMEM = pl.BlockSpec(memory_space=pltpu.SMEM)


def dot(left, right, left_dim=1, right_dim=0):
    return lax.dot_general(
        left, right, (((left_dim,), (right_dim,)), ((), ())), preferred_element_type=f32
    )


def norm_parts(values):
    center = values - jnp.mean(values, axis=-1, keepdims=True)
    spread = jnp.mean(center * center, axis=-1, keepdims=True)
    rate = lax.rsqrt(spread + EPS)
    return center * rate, rate


def norm_back(grad, gain, unit, rate):
    scaled = grad * gain
    first = jnp.mean(scaled, axis=-1, keepdims=True)
    second = jnp.mean(scaled * unit, axis=-1, keepdims=True)
    return rate * (scaled - first - unit * second)


def neighbours():
    place = lax.axis_index("tensor")
    core = place % 2
    chip = place // 2
    return core, chip * 2 + (1 - core), (1 - chip) * 2 + core


def greet(sibling, across, partners=()):
    barrier = pltpu.get_barrier_semaphore()
    for other in (sibling, across):
        pl.semaphore_signal(barrier, inc=1, device_id={"tensor": other}, device_id_type=MESH)
    for other in partners:
        pl.semaphore_signal(barrier, inc=1, device_id={"dp": other}, device_id_type=MESH)
    pl.semaphore_wait(barrier, 2 + len(partners))


def send(source, target, sems, slot, other):
    return pltpu.make_async_remote_copy(
        src_ref=source,
        dst_ref=target,
        send_sem=sems.at[0, slot],
        recv_sem=sems.at[1, slot],
        device_id={"tensor": other},
        device_id_type=MESH,
    )


def row_of(vector):
    return vector[...].reshape(1, vector.shape[0])


def dp_partners(size):
    place = lax.axis_index("dp")
    found = []
    step = 1
    while step < size:
        bit = (place // step) % 2
        found.append((bit, place + (1 - 2 * bit) * step))
        step *= 2
    return found


def halving(length, levels):
    plan = []
    for _ in range(levels):
        halve = (length // 2) % 16 == 0
        plan.append((length, halve))
        length = length // 2 if halve else length
    return plan


def arrivals(length, levels):
    return sum(held // 2 if halve else held for held, halve in halving(length, levels))


class Merge:
    def __init__(self, held, final, arrived, sems, keep_sems, slot, partners, order):
        self.held, self.final, self.arrived = held, final, arrived
        self.sems, self.keep_sems = sems, keep_sems
        self.slot = slot
        self.done = 0
        self.kept = False
        self.steps = []
        length = held.shape[1]
        offset = 0
        place = 0
        for (count, halve), level in zip(halving(length, len(partners)), order):
            bit, partner = partners[level]
            part = count // 2 if halve else count
            keep = offset + bit * part if halve else offset
            give = offset + (1 - bit) * part if halve else offset
            self.steps.append((halve, part, keep, give, place, partner))
            offset = keep
            place += part
        self.last = part

    def where(self, start, count):
        return pl.ds(pl.multiple_of(start, 16), count)

    def own_copy(self):
        where = self.where(self.steps[-1][2], self.last)
        return pltpu.make_async_copy(
            self.held.at[self.slot, where, :],
            self.final.at[self.slot, where, :],
            self.keep_sems.at[self.slot],
        )

    def copy(self, number):
        levels = len(self.steps)
        back = number >= levels
        halve, part, keep, give, place, partner = self.steps[
            2 * levels - 1 - number if back else number
        ]
        if back:
            if not halve:
                return None
            where = self.where(keep, part)
            source = (self.held if part == self.last else self.final).at[self.slot, where, :]
            target = self.final.at[self.slot, where, :]
        else:
            source = self.held.at[self.slot, self.where(give, part), :]
            target = self.arrived.at[self.slot, pl.ds(place, part), :]
        return pltpu.make_async_remote_copy(
            src_ref=source,
            dst_ref=target,
            send_sem=self.sems.at[0, self.slot, number],
            recv_sem=self.sems.at[1, self.slot, number],
            device_id={"dp": partner},
            device_id_type=MESH,
        )

    def start(self):
        copy = self.copy(self.done)
        if copy is not None:
            copy.start()

    def finished(self):
        return self.done == 2 * len(self.steps)

    def advance(self):
        levels = len(self.steps)
        if self.finished():
            return
        number = self.done
        copy = self.copy(number)
        if copy is not None:
            copy.wait()
        if number < levels:
            _, part, keep, _, place, _ = self.steps[number]
            mine = self.where(keep, part)
            self.held[self.slot, mine, :] = (
                self.held[self.slot, mine, :].astype(f32)
                + self.arrived[self.slot, pl.ds(place, part), :].astype(f32)
            ).astype(bf16)
            if number == levels - 1:
                self.own_copy().start()
        elif copy is not None and not self.kept:
            self.own_copy().wait()
            self.kept = True
        self.done += 1
        if not self.finished():
            self.start()


def rows(start, count):
    return pl.ds(pl.multiple_of(start, count), count)


def item_ends(lengths_ref):
    ends = []
    total = 0
    for slot in range(lengths_ref.shape[1]):
        total = total + lengths_ref[0, slot]
        ends.append(total)
    return ends


def item_at(place, ends):
    item = jnp.zeros(place.shape, jnp.int32)
    for end in ends:
        item = item + (place >= end).astype(jnp.int32)
    return item


def mask_tile(ends, visible, row_start, count, key_start, keys):
    row = row_start + lax.broadcasted_iota(jnp.int32, (count, 1), 0)
    key = key_start + lax.broadcasted_iota(jnp.int32, (1, keys), 1)
    allowed = (item_at(row, ends) == item_at(key, ends)) & ((visible == 1) | (row == key))
    return jnp.where(allowed, 0.0, MASKED).astype(f32)


def head_lanes(head, kind):
    lane = lax.broadcasted_iota(jnp.int32, (1, LANES), 1)
    return ((lane >= head * HEAD_DIM) & (lane < (head + 1) * HEAD_DIM)).astype(f32).astype(kind)


def spread_columns(heads, part):
    source = lax.broadcasted_iota(jnp.int32, (heads * 3 * HEAD_DIM, 1), 0)
    inside = lax.broadcasted_iota(jnp.int32, (1, LANES), 1)
    wanted = (inside // HEAD_DIM) * (3 * HEAD_DIM) + part * HEAD_DIM + inside % HEAD_DIM
    wanted = jnp.where(inside < heads * HEAD_DIM, wanted, -1)
    return (source == wanted).astype(f32).astype(bf16)


def valid_rows(ends, start, count):
    row = start + lax.broadcasted_iota(jnp.int32, (count, 1), 0)
    return (row < ends[-1]).astype(f32)


SCALE = HEAD_DIM ** (-0.5)


class Sum:
    def __init__(self, part, from_core, chip_sum, from_chip, sems, core, sibling, across):
        self.part, self.from_core, self.chip_sum, self.from_chip = (
            part,
            from_core,
            chip_sum,
            from_chip,
        )
        self.sems = sems
        self.core, self.sibling, self.across = core, sibling, across

    def ours(self, block):
        return rows(block * SPAN + self.core * HALF, HALF)

    def theirs(self, block):
        return rows(block * SPAN + (1 - self.core) * HALF, HALF)

    def copy(self, source, target, stage, block, other):
        return pltpu.make_async_remote_copy(
            src_ref=source,
            dst_ref=target,
            send_sem=self.sems.at[0, stage, block],
            recv_sem=self.sems.at[1, stage, block],
            device_id={"tensor": other},
            device_id_type=MESH,
        )

    def to_core(self, block):
        return self.copy(
            self.part.at[self.theirs(block), :], self.from_core(block), 0, block, self.sibling
        )

    def to_chip(self, block):
        return self.copy(
            self.chip_sum(block), self.from_chip.at[block], 1, block, self.across
        )

    def share(self, block, source, target):
        return self.copy(source, target.at[self.ours(block), :], 2, block, self.sibling)

    def cross(self, block):
        self.to_core(block).wait()
        mine = self.part[self.ours(block), :].astype(f32)
        self.chip_sum(block)[...] = (mine + self.from_core(block)[...].astype(f32)).astype(bf16)
        self.to_chip(block).start()

    def result(self, block):
        self.to_chip(block).wait()
        return self.chip_sum(block)[...].astype(f32) + self.from_chip[block].astype(f32)


def merge_order(number, levels):
    near = list(range(levels))
    return near[1:] + near[:1] if number == 1 else near


def layer_kernel(
    heads,
    dp,
    tokens,
    attend_weight,
    attend_bias,
    mixing_weight,
    mixing_bias,
    first_gain,
    first_shift,
    second_gain,
    second_shift,
    expand_bias,
    shrink_bias,
    visible,
    lengths,
    expand_source,
    shrink_source,
    cotangent_source,
    layer_output,
    input_grad,
    grads,
    small,
    expand_weight,
    shrink_weight,
    cotangent,
    normed,
    joined,
    wide_weight,
    context,
    log_totals,
    middle,
    middle_back,
    wide_mixing,
    bias,
    seen,
    masks,
    ffn_in,
    act,
    hidden_back,
    ffn_back,
    attn_back,
    key_grad,
    value_grad,
    part,
    from_core,
    chip_sum,
    from_chip,
    norm2_from_chip,
    norm1_from_chip,
    held,
    arrived,
    small_sum,
    small_in,
    attn_sems,
    norm2_sems,
    norm1_sems,
    out_sems,
    merge_sems,
    keep_sems,
    small_sems,
    load_sems,
    output_sems,
    input_sems,
):
    core, sibling, across = neighbours()
    partners = dp_partners(dp)
    levels = len(partners)
    height, depth = tokens.shape
    units = expand_weight.shape[1]
    blocks = height // SPAN
    width = heads * HEAD_DIM
    last = grads.shape[0] - 1
    ends = item_ends(lengths)
    loads = [
        pltpu.make_async_copy(source, target, load_sems.at[number])
        for number, (source, target) in enumerate(
            (
                (expand_source, expand_weight),
                (shrink_source, shrink_weight),
                (cotangent_source, cotangent),
            )
        )
    ]
    for load in loads:
        load.start()
    greet(sibling, across, [partner for _, partner in partners])
    place3 = (core, sibling, across)
    from_core_at = lambda block: from_core.at[block]
    chip_sum_at = lambda block: chip_sum.at[block]

    def late_from_core(block):
        buffer = act if block == 1 else hidden_back
        lanes = slice(depth, 2 * depth) if block == 2 else slice(0, depth)
        return buffer.at[heads * HALF : heads * HALF + HALF, lanes]

    def late_chip_sum(block):
        return ffn_in.at[rows(block * SPAN + (1 - core) * HALF, HALF), :]

    attn = Sum(part, from_core_at, chip_sum_at, from_chip, attn_sems, *place3)
    norm2 = Sum(part, from_core_at, chip_sum_at, norm2_from_chip, norm2_sems, *place3)
    norm1 = Sum(part, late_from_core, late_chip_sum, norm1_from_chip, norm1_sems, *place3)
    out_part = ffn_back
    out = Sum(out_part, from_core_at, chip_sum_at, from_chip, out_sems, *place3)
    merges = [
        Merge(
            held,
            grads,
            arrived,
            merge_sems,
            keep_sems,
            number,
            partners,
            merge_order(number, levels),
        )
        for number in range(last + 1)
    ]

    def begin(number):
        merges[number].start()

    def push(*numbers):
        for number in numbers:
            merges[number].advance()

    def own(block):
        return slice(block * HALF, (block + 1) * HALF)


    for number in range(3):
        lanes = slice(number * LANES, (number + 1) * LANES)
        wide_weight[lanes, :] = dot(
            spread_columns(heads, number), attend_weight[...], 0, 0
        ).astype(bf16)
    seen[...] = row_of(visible)
    blank = jnp.zeros((1, LANES - width), f32)
    for part_at, lane_at in ((0, 0), (2, HEAD_DIM)):
        pieces = [attend_bias[h : h + 1, lane_at : lane_at + HEAD_DIM] for h in range(heads)]
        bias[:, part_at * LANES : (part_at + 1) * LANES] = jnp.concatenate(
            pieces + [blank], axis=1
        )
    bias[:, LANES : 2 * LANES] = jnp.zeros((1, LANES), f32)
    wide_mixing[...] = jnp.zeros_like(wide_mixing)
    wide_mixing[0:width, :] = mixing_weight[...]
    small[...] = jnp.zeros_like(small)

    def collect(number, values):
        small[number : number + 1, 0 : values.shape[1]] += jnp.sum(values, axis=0, keepdims=True)

    def project_step(step, carry):
        where = rows(step * HALF, HALF)
        unit, _ = norm_parts(tokens[where, :].astype(f32))
        fresh = (unit * row_of(first_gain) + row_of(first_shift)).astype(bf16)
        normed[where, :] = fresh
        joined[where, :] = (dot(fresh, wide_weight[...], 1, 1) + bias[...]).astype(bf16)
        return carry


    short_tiles = [
        (start, 128, min(start - 64, height - 256), 256) for start in range(WINDOW, height, 128)
    ]

    def dense_tile(step):
        return (pl.multiple_of(step * HALF, HALF), HALF, 0, WINDOW)

    def attend(row_start, count, key_start, keys):
        query = joined[pl.ds(row_start, count), 0:LANES]
        key_rows = pl.ds(key_start, keys)
        key = joined[key_rows, LANES : 2 * LANES]
        value = joined[key_rows, 2 * LANES : 3 * LANES]
        masks[0:count, 0:keys] = mask_tile(
            ends, seen[:, key_rows], row_start, count, key_start, keys
        )
        lane = lax.broadcasted_iota(jnp.int32, (1, 128), 1)
        mixed = jnp.zeros((count, LANES), f32)
        stats = jnp.zeros((count, 128), f32)
        for head in range(heads):
            scores = dot(query * head_lanes(head, bf16), key, 1, 1)
            scores = scores * (SCALE * LOG2E) + masks[0:count, 0:keys]
            top = jnp.max(scores, axis=-1, keepdims=True)
            powers = jnp.exp2(scores - top)
            total = jnp.sum(powers, axis=-1, keepdims=True)
            mine = dot(powers.astype(bf16), value) / total
            mixed = mixed + mine * head_lanes(head, f32)
            stats = jnp.where(lane == head, top + jnp.log2(total), stats)
        context[pl.ds(row_start, count), :] = mixed.astype(bf16)
        log_totals[pl.ds(row_start, count), :] = stats

    def dense(first, stop):
        def step(number, carry):
            attend(*dense_tile(number))
            return carry

        lax.fori_loop(first, stop, step, 0)

    def mix(block):
        for half in range(2):
            where = slice(block * SPAN + half * HALF, block * SPAN + (half + 1) * HALF)
            part[where, :] = dot(context[where, :], wide_mixing[...]).astype(bf16)
        attn.to_core(block).start()

    def attn_share(block):
        where = attn.ours(block)
        return attn.share(block, ffn_in.at[where, :], ffn_in)

    def finish_attn(block):
        total = attn.result(block)
        where = attn.ours(block)
        center = tokens[where, :].astype(f32) + (total + row_of(mixing_bias)) * valid_rows(
            ends, block * SPAN + core * HALF, HALF
        )
        middle[own(block), :] = center
        unit, _ = norm_parts(center)
        ffn_in[where, :] = (unit * row_of(second_gain) + row_of(second_shift)).astype(bf16)
        attn_share(block).start()


    halves = [slice(n * depth, (n + 1) * depth) for n in range(units // depth)]

    def mask_back(where, start):
        back = (cotangent[where, :].astype(f32) * valid_rows(ends, start, HALF)).astype(bf16)
        ffn_back[where, :] = back
        collect(0, back.astype(f32))

    def forward(where, columns):
        hidden = dot(ffn_in[where, :], expand_weight[:, columns])
        hidden = hidden + row_of(expand_bias)[:, columns]
        smooth = 0.5 + 0.5 * lax.erf(hidden * (0.5**0.5))
        act[where, columns] = (hidden * smooth).astype(bf16)
        return smooth + hidden * (
            0.3989422804014327 * jnp.exp2(hidden * hidden * (-0.5 * LOG2E))
        )

    def backward(where, number, slope):
        columns = halves[number]
        fresh = (slope * dot(ffn_back[where, :], shrink_weight[columns, :], 1, 1)).astype(bf16)
        hidden_back[where, columns] = fresh
        collect(1 + number, fresh.astype(f32))

    def place(block, theirs):
        start = block * SPAN + (1 - core if theirs else core) * HALF
        return rows(start, HALF), start

    def pass_back(block, theirs):
        where, _ = place(block, theirs)
        part[where, :] = dot(hidden_back[where, :], expand_weight[...], 1, 1).astype(bf16)
        if theirs:
            norm2.to_core(block).start()

    def feed(block, theirs):
        where, start = place(block, theirs)
        mask_back(where, start)
        for number, columns in enumerate(halves):
            backward(where, number, forward(where, columns))
        pass_back(block, theirs)

    def feed_forward(block, theirs):
        where, start = place(block, theirs)
        mask_back(where, start)
        for columns in halves:
            hidden_back[where, columns] = forward(where, columns).astype(bf16)

    def feed_back(block, theirs):
        where, _ = place(block, theirs)
        for number, columns in enumerate(halves):
            backward(where, number, hidden_back[where, columns].astype(f32))
        pass_back(block, theirs)

    def add_out(block):
        for half in range(2):
            where = slice(block * SPAN + half * HALF, block * SPAN + (half + 1) * HALF)
            out_part[where, :] = dot(act[where, :], shrink_weight[...]).astype(bf16)
        out.to_core(block).start()

    def norm2_share(block):
        return norm2.share(block, attn_back.at[norm2.ours(block), :], attn_back)

    def finish_norm2(block):
        grad = norm2.result(block)
        unit, rate = norm_parts(middle[own(block), :])
        collect(3, grad * unit)
        collect(4, grad)
        where = norm2.ours(block)
        full = cotangent[where, :].astype(f32) + norm_back(
            grad, row_of(second_gain), unit, rate
        )
        middle_back[own(block), :] = full
        attn_back[where, :] = (
            full * valid_rows(ends, block * SPAN + core * HALF, HALF)
        ).astype(bf16)
        norm2_share(block).start()


    score_stack = hidden_back
    prob_stack = act
    spare = slice(WINDOW, WINDOW + LANES)
    joined_back = joined

    def turn_back(block):
        where = slice(block * SPAN, (block + 1) * SPAN)
        act[where, spare] = dot(attn_back[where, :], wide_mixing[...], 1, 1).astype(bf16)
        collect(5, attn_back[where, :].astype(f32))

    def attend_back(row_start, count, key_start, keys):
        where = pl.ds(row_start, count)
        key_rows = pl.ds(key_start, keys)
        query = joined[where, 0:LANES]
        back = act[where, spare]
        overlap = back.astype(f32) * context[where, :].astype(f32)
        masks[0:count, 0:keys] = mask_tile(
            ends, seen[:, key_rows], row_start, count, key_start, keys
        )
        query_grad = jnp.zeros((count, LANES), f32)
        step = min(keys, SPAN)
        for head in range(heads):
            mine = head_lanes(head, bf16)
            head_rows = slice(head * count, (head + 1) * count)
            delta = jnp.sum(overlap * head_lanes(head, f32), axis=-1, keepdims=True)
            log_total = log_totals[where, head : head + 1]
            found = jnp.zeros((count, LANES), f32)
            for start in range(0, keys, step):
                chunk = slice(start, start + step)
                chunk_rows = pl.ds(key_start + start, step)
                key = joined[chunk_rows, LANES : 2 * LANES]
                value = joined[chunk_rows, 2 * LANES : 3 * LANES]
                scores = dot(query * mine, key, 1, 1)
                scores = scores * (SCALE * LOG2E) + masks[0:count, chunk]
                probs = jnp.exp2(scores - log_total)
                prob_stack[head_rows, chunk] = probs.astype(bf16)
                change = probs * (dot(back * mine, value, 1, 1) - delta)
                low_change = change.astype(bf16)
                score_stack[head_rows, chunk] = low_change
                found = found + dot(low_change, key)
            query_grad = query_grad + found * head_lanes(head, f32)
        query_low = (query_grad * SCALE).astype(bf16)
        joined_back[where, 0:LANES] = query_low
        collect(6, query_low.astype(f32))
        many_query = jnp.concatenate([query * head_lanes(h, bf16) for h in range(heads)], axis=0)
        many_back = jnp.concatenate([back * head_lanes(h, bf16) for h in range(heads)], axis=0)
        key_grad[key_rows, :] += dot(score_stack[0 : heads * count, 0:keys], many_query, 0, 0)
        value_grad[key_rows, :] += dot(prob_stack[0 : heads * count, 0:keys], many_back, 0, 0)

    def dense_back(first, stop):
        def step(number, carry):
            attend_back(*dense_tile(number))
            return carry

        lax.fori_loop(first, stop, step, 0)

    def project_back(block):
        for half in range(2):
            where = slice(block * SPAN + half * HALF, block * SPAN + (half + 1) * HALF)
            joined_back[where, LANES : 2 * LANES] = (key_grad[where, :] * SCALE).astype(bf16)
            value_low = value_grad[where, :].astype(bf16)
            joined_back[where, 2 * LANES : 3 * LANES] = value_low
            small[6:7, LANES : 2 * LANES] += jnp.sum(
                value_low.astype(f32), axis=0, keepdims=True
            )
            part[where, :] = dot(joined_back[where, :], wide_weight[...]).astype(bf16)
        norm1.to_core(block).start()

    def input_copies(block):
        source = middle_back.at[own(block), :]
        return (
            norm1.share(block, source, input_grad),
            pltpu.make_async_copy(
                source, input_grad.at[norm1.ours(block), :], input_sems.at[block]
            ),
        )

    def finish_norm1(block):
        grad = norm1.result(block)
        unit, rate = norm_parts(tokens[norm1.ours(block), :].astype(f32))
        collect(7, grad * unit)
        collect(8, grad)
        middle_back[own(block), :] += norm_back(grad, row_of(first_gain), unit, rate)
        for copy in input_copies(block):
            copy.start()

    def output_copies(block):
        where = out.ours(block)
        return (
            out.share(block, ffn_in.at[where, :], layer_output),
            pltpu.make_async_copy(
                ffn_in.at[where, :], layer_output.at[where, :], output_sems.at[block]
            ),
        )

    def finish_out(block):
        total = out.result(block) + row_of(shrink_bias)
        ffn_in[out.ours(block), :] = (
            middle[own(block), :]
            + total * valid_rows(ends, block * SPAN + core * HALF, HALF)
        ).astype(bf16)
        for copy in output_copies(block):
            copy.start()


    steps = height // HALF
    first = WINDOW // HALF - 1
    lax.fori_loop(first, steps, project_step, 0)
    for tile in short_tiles:
        attend(*tile)
    mix(2)
    lax.fori_loop(0, first, project_step, 0)
    attn.cross(2)
    dense(0, 2)
    mix(0)
    dense(2, 3)
    attn.cross(0)
    dense(3, 4)
    mix(1)
    finish_attn(2)
    attn.cross(1)
    for load in loads:
        load.wait()
    attn_share(2).wait()
    feed(2, True)
    feed(2, False)
    finish_attn(0)
    norm2.cross(2)
    attn_share(0).wait()
    feed(0, True)
    feed(0, False)
    finish_attn(1)
    norm2.cross(0)
    attn_share(1).wait()
    feed_forward(1, True)
    feed_forward(1, False)
    for number, columns in enumerate(halves):
        held[number] = dot(act[:, columns], ffn_back[...], 0, 0).astype(bf16)
        begin(number)
    feed_back(1, True)
    feed_back(1, False)
    norm2.cross(1)
    for number, columns in enumerate(halves):
        held[2 + number] = dot(ffn_in[...], hidden_back[:, columns], 0, 0).astype(bf16)
    finish_norm2(2)
    push(0)
    begin(2)
    key_grad[...] = jnp.zeros_like(key_grad)
    value_grad[...] = jnp.zeros_like(value_grad)
    norm2_share(2).wait()
    for block in (2, 0, 1):
        add_out(block)
    turn_back(2)
    push(1)
    for tile in short_tiles[:2]:
        attend_back(*tile)
    push(0)
    for tile in short_tiles[2:]:
        attend_back(*tile)
    project_back(2)
    finish_norm2(0)
    push(2)
    begin(3)
    norm2_share(0).wait()
    turn_back(0)
    norm1.cross(2)
    dense_back(0, 1)
    push(0, 1)
    push(2)
    dense_back(1, 2)
    finish_norm2(1)
    push(1, 0)
    out.cross(2)
    norm2_share(1).wait()
    turn_back(1)
    dense_back(2, 3)
    push(3)
    push(1, 0, 2)
    dense_back(3, 4)
    project_back(0)
    project_back(1)
    push(3)
    held[last, 3 * width : 4 * width, :] = dot(context[...], attn_back[...], 0, 0)[
        0:width, :
    ].astype(bf16)
    norm1.cross(0)
    for number in range(3):
        lanes = slice(number * LANES, (number + 1) * LANES)
        wide = dot(joined_back[:, lanes], normed[...], 0, 0).astype(bf16)
        placed = dot(spread_columns(heads, number), wide)
        if number > 0:
            placed = placed + held[last, 0 : 3 * width, :].astype(f32)
        held[last, 0 : 3 * width, :] = placed.astype(bf16)
    begin(last)
    norm1.cross(1)
    out.cross(0)
    out.cross(1)
    push(2, 3, 1, 0)
    finish_norm1(2)
    push(3, 1)
    finish_out(2)
    push(2, last)
    finish_norm1(0)
    push(last)
    finish_norm1(1)
    push(2, 3, last)
    small[9:10, :] = jnp.full((1, depth), ends[-1], jnp.int32).astype(f32)
    small_sum[0] = small[...]
    copy = send(small_sum.at[0], small_in.at[0], small_sems, 0, sibling)
    copy.start()
    copy.wait()
    line = lax.broadcasted_iota(jnp.int32, (16, 1), 0)
    both = (line == 3) | (line == 4) | (line == 7) | (line == 8)
    small_sum[1] = small_sum[0] + jnp.where(both, small_in[0], 0.0)
    for level in range(levels):
        copy = pltpu.make_async_remote_copy(
            src_ref=small_sum.at[1 + level],
            dst_ref=small_in.at[1 + level],
            send_sem=small_sems.at[0, 1 + level],
            recv_sem=small_sems.at[1, 1 + level],
            device_id={"dp": partners[level][1]},
            device_id_type=MESH,
        )
        copy.start()
        copy.wait()
        small_sum[2 + level] = small_sum[1 + level] + small_in[1 + level]
    small[...] = small_sum[1 + levels]
    push(last)
    finish_out(0)
    finish_out(1)
    while not all(merge.finished() for merge in merges):
        push(*range(last + 1))
    for block in range(blocks):
        for copy in input_copies(block) + output_copies(block):
            copy.wait()


def final_kernel(
    heads,
    dp,
    grads,
    small,
    attend_grad,
    attend_bias_grad,
    mixing_grad,
    mixing_bias_grad,
    expand_grad,
    expand_bias_grad,
    shrink_grad,
    shrink_bias_grad,
    first_gain_grad,
    first_shift_grad,
    second_gain_grad,
    second_shift_grad,
    stage,
    sems,
):
    width = heads * HEAD_DIM
    depth = grads.shape[1]
    factor = dp / small[9:10, :]
    last = grads.shape[0] - 1
    copies = []
    targets = (
        (0, 0, depth, shrink_grad.at[0:depth, :]),
        (1, 0, depth, shrink_grad.at[depth : 2 * depth, :]),
        (2, 0, depth, expand_grad.at[:, 0:depth]),
        (3, 0, depth, expand_grad.at[:, depth : 2 * depth]),
        (last, 0, 3 * width, attend_grad),
        (last, 3 * width, width, mixing_grad),
    )
    for index, (number, start, count, target) in enumerate(targets):
        stage[number, start : start + count, :] = (
            grads[number, start : start + count, :].astype(f32) * factor
        )
        copy = pltpu.make_async_copy(
            stage.at[number, start : start + count, :], target, sems.at[index]
        )
        copy.start()
        copies.append(copy)

    def line(number):
        return small[number : number + 1, :] * factor

    for target, number in (
        (shrink_bias_grad, 0),
        (second_gain_grad, 3),
        (second_shift_grad, 4),
        (mixing_bias_grad, 5),
        (first_gain_grad, 7),
        (first_shift_grad, 8),
    ):
        target[...] = line(number).reshape(depth)
    for number in range(2):
        expand_bias_grad[number * depth : (number + 1) * depth] = line(1 + number).reshape(depth)
    both = line(6)
    for head in range(heads):
        for at, lane in ((0, 0), (LANES, HEAD_DIM)):
            first = at + head * HEAD_DIM
            attend_bias_grad[head : head + 1, lane : lane + HEAD_DIM] = both[
                :, first : first + HEAD_DIM
            ]
    for copy in copies:
        copy.wait()


def shape(*dims, kind=bf16):
    return jax.ShapeDtypeStruct(dims, kind)


def params(number):
    return pltpu.CompilerParams(
        collective_id=number, has_side_effects=True, vmem_limit_bytes=63 * 2**20
    )


def sems(blocks):
    return pltpu.SemaphoreType.DMA((2, blocks))


def per_device(
    tokens,
    attend_weight,
    attend_bias,
    mixing_weight,
    mixing_bias,
    expand_weight,
    expand_bias,
    shrink_weight,
    shrink_bias,
    first_gain,
    first_shift,
    second_gain,
    second_shift,
    item_lengths,
    visible,
    cotangent,
):
    height, depth = tokens.shape
    heads = attend_bias.shape[0]
    units = expand_weight.shape[1]
    width = heads * HEAD_DIM
    blocks = height // SPAN
    own = height // 2
    dp = lax.axis_size("dp")
    levels = dp.bit_length() - 1
    chunks = 1 + 2 * units // depth
    low = lambda *dims: pltpu.VMEM(dims, bf16)
    high = lambda *dims: pltpu.VMEM(dims, f32)
    block_buffer = low(blocks, HALF, depth)
    sum_sems = pltpu.SemaphoreType.DMA((2, 3, blocks))

    layer_output, input_grad, grads, small = pl.pallas_call(
        functools.partial(layer_kernel, heads, dp),
        out_shape=(
            shape(height, depth),
            shape(height, depth, kind=f32),
            shape(chunks, depth, depth),
            shape(16, depth, kind=f32),
        ),
        in_specs=[VMEM] * 12 + [SMEM] + [ANY] * 3,
        out_specs=(ANY, ANY, ANY, VMEM),
        scratch_shapes=[
            low(depth, units),
            low(units, depth),
            low(height, depth),
            low(height, depth),
            low(height, 3 * LANES),
            low(3 * LANES, depth),
            low(height, LANES),
            high(height, 128),
            high(own, depth),
            high(own, depth),
            low(LANES, depth),
            high(1, 3 * LANES),
            pltpu.VMEM((1, height), jnp.int32),
            high(HALF, WINDOW),
            low(height, depth),
            low(height, units),
            low(height, units),
            low(height, depth),
            low(height, depth),
            high(height, LANES),
            high(height, LANES),
            low(height, depth),
            block_buffer,
            block_buffer,
            block_buffer,
            block_buffer,
            block_buffer,
            low(chunks, depth, depth),
            low(chunks, arrivals(depth, levels), depth),
            high(levels + 2, 16, depth),
            high(levels + 2, 16, depth),
            sum_sems,
            sum_sems,
            sum_sems,
            sum_sems,
            pltpu.SemaphoreType.DMA((2, chunks, 2 * levels)),
            pltpu.SemaphoreType.DMA((chunks,)),
            sems(1 + levels),
            pltpu.SemaphoreType.DMA((3,)),
            pltpu.SemaphoreType.DMA((blocks,)),
            pltpu.SemaphoreType.DMA((blocks,)),
        ],
        compiler_params=params(0),
        name="layer",
    )(
        tokens,
        attend_weight.T,
        attend_bias,
        mixing_weight,
        mixing_bias,
        first_gain,
        first_shift,
        second_gain,
        second_shift,
        expand_bias,
        shrink_bias,
        visible,
        item_lengths,
        expand_weight,
        shrink_weight,
        cotangent,
    )

    vector = shape(depth, kind=f32)
    outs = pl.pallas_call(
        functools.partial(final_kernel, heads, dp),
        out_shape=(
            shape(3 * width, depth, kind=f32),
            shape(heads, 2 * HEAD_DIM, kind=f32),
            shape(width, depth, kind=f32),
            vector,
            shape(depth, units, kind=f32),
            shape(units, kind=f32),
            shape(units, depth, kind=f32),
            vector,
            vector,
            vector,
            vector,
            vector,
        ),
        in_specs=[VMEM] * 2,
        out_specs=(ANY, VMEM, ANY, VMEM, ANY, VMEM, ANY) + (VMEM,) * 5,
        scratch_shapes=[
            pltpu.VMEM((chunks, depth, depth), f32),
            pltpu.SemaphoreType.DMA((6,)),
        ],
        compiler_params=pltpu.CompilerParams(vmem_limit_bytes=40 * 2**20),
        name="final",
    )(grads, small)
    return (layer_output, input_grad, outs[0].T) + tuple(outs[1:])


def solution(mesh):
    placed = (
        P("dp", None),
        P(None, "tensor"),
        P("tensor", None),
        P("tensor", None),
        P(),
        P(None, "tensor"),
        P("tensor"),
        P("tensor", None),
        P(),
        P(),
        P(),
        P(),
        P(),
        P("dp", None),
        P("dp"),
        P("dp", None),
    )
    return jax.shard_map(
        per_device,
        mesh=mesh,
        in_specs=placed,
        out_specs=(
            P("dp", None),
            P("dp", None),
            P(None, "tensor"),
            P("tensor", None),
            P("tensor", None),
            P(),
            P(None, "tensor"),
            P("tensor"),
            P("tensor", None),
            P(),
            P(),
            P(),
            P(),
            P(),
        ),
        check_vma=False,
    )
```

```python
import functools

import jax
import jax.numpy as jnp
from jax import lax
from jax.experimental import pallas as pl
from jax.experimental.pallas import tpu as pltpu
from jax.sharding import PartitionSpec as P

HEAD_DIM = 32
LANES = 256
SPAN = 512
HALF = SPAN // 2
WINDOW = 1024
EPS = 1e-05
LOG2E = 1.4426950408889634
MASKED = -1e30
MESH = pl.DeviceIdType.MESH
f32 = jnp.float32
bf16 = jnp.bfloat16
VMEM = pl.BlockSpec(memory_space=pltpu.VMEM)
ANY = pl.BlockSpec(memory_space=pl.ANY)
SMEM = pl.BlockSpec(memory_space=pltpu.SMEM)


def dot(left, right, left_dim=1, right_dim=0):
    return lax.dot_general(
        left, right, (((left_dim,), (right_dim,)), ((), ())), preferred_element_type=f32
    )


def norm_parts(values):
    center = values - jnp.mean(values, axis=-1, keepdims=True)
    spread = jnp.mean(center * center, axis=-1, keepdims=True)
    rate = lax.rsqrt(spread + EPS)
    return center * rate, rate


def norm_back(grad, gain, unit, rate):
    scaled = grad * gain
    first = jnp.mean(scaled, axis=-1, keepdims=True)
    second = jnp.mean(scaled * unit, axis=-1, keepdims=True)
    return rate * (scaled - first - unit * second)


def neighbours():
    place = lax.axis_index("tensor")
    core = place % 2
    chip = place // 2
    return core, chip * 2 + (1 - core), (1 - chip) * 2 + core


def greet(sibling, across, partners=()):
    barrier = pltpu.get_barrier_semaphore()
    for other in (sibling, across):
        pl.semaphore_signal(barrier, inc=1, device_id={"tensor": other}, device_id_type=MESH)
    for other in partners:
        pl.semaphore_signal(barrier, inc=1, device_id={"dp": other}, device_id_type=MESH)
    pl.semaphore_wait(barrier, 2 + len(partners))


def send(source, target, sems, slot, other):
    return pltpu.make_async_remote_copy(
        src_ref=source,
        dst_ref=target,
        send_sem=sems.at[0, slot],
        recv_sem=sems.at[1, slot],
        device_id={"tensor": other},
        device_id_type=MESH,
    )


def row_of(vector):
    return vector[...].reshape(1, vector.shape[0])


def dp_partners(size):
    place = lax.axis_index("dp")
    found = []
    step = 1
    while step < size:
        bit = (place // step) % 2
        found.append((bit, place + (1 - 2 * bit) * step))
        step *= 2
    return found


def halving(length, levels):
    plan = []
    for _ in range(levels):
        halve = (length // 2) % 16 == 0
        plan.append((length, halve))
        length = length // 2 if halve else length
    return plan


def arrivals(length, levels):
    return sum(held // 2 if halve else held for held, halve in halving(length, levels))


class Merge:
    def __init__(self, held, final, arrived, sems, keep_sems, slot, partners, order):
        self.held, self.final, self.arrived = held, final, arrived
        self.sems, self.keep_sems = sems, keep_sems
        self.slot = slot
        self.done = 0
        self.kept = False
        self.steps = []
        length = held.shape[1]
        offset = 0
        place = 0
        for (count, halve), level in zip(halving(length, len(partners)), order):
            bit, partner = partners[level]
            part = count // 2 if halve else count
            keep = offset + bit * part if halve else offset
            give = offset + (1 - bit) * part if halve else offset
            self.steps.append((halve, part, keep, give, place, partner))
            offset = keep
            place += part
        self.last = part

    def where(self, start, count):
        return pl.ds(pl.multiple_of(start, 16), count)

    def own_copy(self):
        where = self.where(self.steps[-1][2], self.last)
        return pltpu.make_async_copy(
            self.held.at[self.slot, where, :],
            self.final.at[self.slot, where, :],
            self.keep_sems.at[self.slot],
        )

    def copy(self, number):
        levels = len(self.steps)
        back = number >= levels
        halve, part, keep, give, place, partner = self.steps[
            2 * levels - 1 - number if back else number
        ]
        if back:
            if not halve:
                return None
            where = self.where(keep, part)
            source = (self.held if part == self.last else self.final).at[self.slot, where, :]
            target = self.final.at[self.slot, where, :]
        else:
            source = self.held.at[self.slot, self.where(give, part), :]
            target = self.arrived.at[self.slot, pl.ds(place, part), :]
        return pltpu.make_async_remote_copy(
            src_ref=source,
            dst_ref=target,
            send_sem=self.sems.at[0, self.slot, number],
            recv_sem=self.sems.at[1, self.slot, number],
            device_id={"dp": partner},
            device_id_type=MESH,
        )

    def start(self):
        copy = self.copy(self.done)
        if copy is not None:
            copy.start()

    def finished(self):
        return self.done == 2 * len(self.steps)

    def advance(self):
        levels = len(self.steps)
        if self.finished():
            return
        number = self.done
        copy = self.copy(number)
        if copy is not None:
            copy.wait()
        if number < levels:
            _, part, keep, _, place, _ = self.steps[number]
            mine = self.where(keep, part)
            self.held[self.slot, mine, :] = (
                self.held[self.slot, mine, :].astype(f32)
                + self.arrived[self.slot, pl.ds(place, part), :].astype(f32)
            ).astype(bf16)
            if number == levels - 1:
                self.own_copy().start()
        elif copy is not None and not self.kept:
            self.own_copy().wait()
            self.kept = True
        self.done += 1
        if not self.finished():
            self.start()


def rows(start, count):
    return pl.ds(pl.multiple_of(start, count), count)


def item_ends(lengths_ref):
    ends = []
    total = 0
    for slot in range(lengths_ref.shape[1]):
        total = total + lengths_ref[0, slot]
        ends.append(total)
    return ends


def item_at(place, ends):
    item = jnp.zeros(place.shape, jnp.int32)
    for end in ends:
        item = item + (place >= end).astype(jnp.int32)
    return item


def mask_tile(ends, visible, row_start, count, key_start, keys):
    row = row_start + lax.broadcasted_iota(jnp.int32, (count, 1), 0)
    key = key_start + lax.broadcasted_iota(jnp.int32, (1, keys), 1)
    allowed = (item_at(row, ends) == item_at(key, ends)) & ((visible == 1) | (row == key))
    return jnp.where(allowed, 0.0, MASKED).astype(f32)


def head_lanes(head, kind):
    lane = lax.broadcasted_iota(jnp.int32, (1, LANES), 1)
    return ((lane >= head * HEAD_DIM) & (lane < (head + 1) * HEAD_DIM)).astype(f32).astype(kind)


def spread_columns(heads, part):
    source = lax.broadcasted_iota(jnp.int32, (heads * 3 * HEAD_DIM, 1), 0)
    inside = lax.broadcasted_iota(jnp.int32, (1, LANES), 1)
    wanted = (inside // HEAD_DIM) * (3 * HEAD_DIM) + part * HEAD_DIM + inside % HEAD_DIM
    wanted = jnp.where(inside < heads * HEAD_DIM, wanted, -1)
    return (source == wanted).astype(f32).astype(bf16)


def valid_rows(ends, start, count):
    row = start + lax.broadcasted_iota(jnp.int32, (count, 1), 0)
    return (row < ends[-1]).astype(f32)


SCALE = HEAD_DIM ** (-0.5)


class Sum:
    def __init__(self, part, from_core, chip_sum, from_chip, sems, core, sibling, across):
        self.part, self.from_core, self.chip_sum, self.from_chip = (
            part,
            from_core,
            chip_sum,
            from_chip,
        )
        self.sems = sems
        self.core, self.sibling, self.across = core, sibling, across

    def ours(self, block):
        return rows(block * SPAN + self.core * HALF, HALF)

    def theirs(self, block):
        return rows(block * SPAN + (1 - self.core) * HALF, HALF)

    def copy(self, source, target, stage, block, other):
        return pltpu.make_async_remote_copy(
            src_ref=source,
            dst_ref=target,
            send_sem=self.sems.at[0, stage, block],
            recv_sem=self.sems.at[1, stage, block],
            device_id={"tensor": other},
            device_id_type=MESH,
        )

    def to_core(self, block):
        return self.copy(
            self.part.at[self.theirs(block), :], self.from_core(block), 0, block, self.sibling
        )

    def to_chip(self, block):
        return self.copy(
            self.chip_sum(block), self.from_chip(block), 1, block, self.across
        )

    def share(self, block, source, target):
        return self.copy(source, target.at[self.ours(block), :], 2, block, self.sibling)

    def cross(self, block):
        self.to_core(block).wait()
        mine = self.part[self.ours(block), :].astype(f32)
        self.chip_sum(block)[...] = (mine + self.from_core(block)[...].astype(f32)).astype(bf16)
        self.to_chip(block).start()

    def result(self, block):
        self.to_chip(block).wait()
        return self.chip_sum(block)[...].astype(f32) + self.from_chip(block)[...].astype(f32)


def merge_order(number, levels):
    near = list(range(levels))
    return near[1:] + near[:1] if number == 1 else near


def layer_kernel(
    heads,
    dp,
    tokens,
    attend_weight,
    attend_bias,
    mixing_weight,
    mixing_bias,
    first_gain,
    first_shift,
    second_gain,
    second_shift,
    expand_bias,
    shrink_bias,
    visible,
    lengths,
    expand_source,
    shrink_source,
    cotangent_source,
    layer_output,
    input_grad,
    grads,
    small,
    expand_weight,
    shrink_weight,
    cotangent,
    normed,
    joined,
    wide_weight,
    context,
    log_totals,
    middle,
    middle_back,
    wide_mixing,
    bias,
    seen,
    masks,
    ffn_in,
    act,
    hidden_back,
    ffn_back,
    attn_back,
    key_grad,
    value_grad,
    part,
    from_core,
    chip_sum,
    from_chip,
    norm2_from_chip,
    norm1_from_chip,
    held,
    arrived,
    small_sum,
    small_in,
    attn_sems,
    norm2_sems,
    norm1_sems,
    out_sems,
    merge_sems,
    keep_sems,
    small_sems,
    load_sems,
    output_sems,
    input_sems,
):
    core, sibling, across = neighbours()
    partners = dp_partners(dp)
    levels = len(partners)
    height, depth = tokens.shape
    units = expand_weight.shape[1]
    blocks = height // SPAN
    width = heads * HEAD_DIM
    last = grads.shape[0] - 1
    ends = item_ends(lengths)
    load_pairs = [
        (expand_source, expand_weight),
        (shrink_source, shrink_weight),
        (cotangent_source, ffn_back),
    ]
    for block in range(blocks):
        mine = rows(block * SPAN + core * HALF, HALF)
        load_pairs.append((cotangent_source.at[mine, :], cotangent.at[block]))
    loads = [
        pltpu.make_async_copy(source, target, load_sems.at[number])
        for number, (source, target) in enumerate(load_pairs)
    ]
    for load in loads:
        load.start()
    greet(sibling, across, [partner for _, partner in partners])
    place3 = (core, sibling, across)
    from_core_at = lambda block: from_core.at[block]
    chip_sum_at = lambda block: chip_sum.at[block]

    def late_from_core(block):
        buffer = act if block == 1 else hidden_back
        lanes = slice(depth, 2 * depth) if block == 2 else slice(0, depth)
        return buffer.at[heads * HALF : heads * HALF + HALF, lanes]

    def late_chip_sum(block):
        return ffn_in.at[rows(block * SPAN + (1 - core) * HALF, HALF), :]

    from_chip_at = lambda block: from_chip.at[block]
    norm2_from_chip_at = lambda block: norm2_from_chip.at[block]

    def late_from_chip(block):
        if block == 2:
            return norm1_from_chip.at[...]
        return expand_weight.at[0:HALF, block * depth : (block + 1) * depth]

    attn = Sum(part, from_core_at, chip_sum_at, from_chip_at, attn_sems, *place3)
    norm2 = Sum(part, from_core_at, chip_sum_at, norm2_from_chip_at, norm2_sems, *place3)
    norm1 = Sum(part, late_from_core, late_chip_sum, late_from_chip, norm1_sems, *place3)
    out_part = ffn_back
    out = Sum(out_part, from_core_at, chip_sum_at, from_chip_at, out_sems, *place3)
    merges = [
        Merge(
            held,
            grads,
            arrived,
            merge_sems,
            keep_sems,
            number,
            partners,
            merge_order(number, levels),
        )
        for number in range(last + 1)
    ]

    def begin(number):
        merges[number].start()

    def push(*numbers):
        for number in numbers:
            merges[number].advance()

    def own(block):
        return slice(block * HALF, (block + 1) * HALF)


    for number in range(3):
        lanes = slice(number * LANES, (number + 1) * LANES)
        wide_weight[lanes, :] = dot(
            spread_columns(heads, number), attend_weight[...], 0, 0
        ).astype(bf16)
    seen[...] = row_of(visible)
    blank = jnp.zeros((1, LANES - width), f32)
    for part_at, lane_at in ((0, 0), (2, HEAD_DIM)):
        pieces = [attend_bias[h : h + 1, lane_at : lane_at + HEAD_DIM] for h in range(heads)]
        bias[:, part_at * LANES : (part_at + 1) * LANES] = jnp.concatenate(
            pieces + [blank], axis=1
        )
    bias[:, LANES : 2 * LANES] = jnp.zeros((1, LANES), f32)
    wide_mixing[...] = jnp.zeros_like(wide_mixing)
    wide_mixing[0:width, :] = mixing_weight[...]
    small[...] = jnp.zeros_like(small)

    def collect(number, values):
        small[number : number + 1, 0 : values.shape[1]] += jnp.sum(values, axis=0, keepdims=True)

    def project_step(step, carry):
        where = rows(step * HALF, HALF)
        unit, _ = norm_parts(tokens[where, :].astype(f32))
        fresh = (unit * row_of(first_gain) + row_of(first_shift)).astype(bf16)
        normed[where, :] = fresh
        joined[where, :] = (dot(fresh, wide_weight[...], 1, 1) + bias[...]).astype(bf16)
        return carry


    short_tiles = [
        (start, 128, min(start - 64, height - 256), 256) for start in range(WINDOW, height, 128)
    ]

    def dense_tile(step):
        return (pl.multiple_of(step * HALF, HALF), HALF, 0, WINDOW)

    def attend(row_start, count, key_start, keys):
        query = joined[pl.ds(row_start, count), 0:LANES]
        key_rows = pl.ds(key_start, keys)
        key = joined[key_rows, LANES : 2 * LANES]
        value = joined[key_rows, 2 * LANES : 3 * LANES]
        masks[0:count, 0:keys] = mask_tile(
            ends, seen[:, key_rows], row_start, count, key_start, keys
        )
        lane = lax.broadcasted_iota(jnp.int32, (1, 128), 1)
        mixed = jnp.zeros((count, LANES), f32)
        stats = jnp.zeros((count, 128), f32)
        for head in range(heads):
            scores = dot(query * head_lanes(head, bf16), key, 1, 1)
            scores = scores * (SCALE * LOG2E) + masks[0:count, 0:keys]
            top = jnp.max(scores, axis=-1, keepdims=True)
            powers = jnp.exp2(scores - top)
            total = jnp.sum(powers, axis=-1, keepdims=True)
            mine = dot(powers.astype(bf16), value) / total
            mixed = mixed + mine * head_lanes(head, f32)
            stats = jnp.where(lane == head, top + jnp.log2(total), stats)
        context[pl.ds(row_start, count), :] = mixed.astype(bf16)
        log_totals[pl.ds(row_start, count), :] = stats

    def dense(first, stop):
        def step(number, carry):
            attend(*dense_tile(number))
            return carry

        lax.fori_loop(first, stop, step, 0)

    def mix(block):
        def body(where):
            part[where, :] = dot(context[where, :], wide_mixing[...]).astype(bf16)

        each_half(block, block + 1, body)
        attn.to_core(block).start()

    def attn_share(block):
        where = attn.ours(block)
        return attn.share(block, ffn_in.at[where, :], ffn_in)

    def finish_attn(block):
        total = attn.result(block)
        where = attn.ours(block)
        center = tokens[where, :].astype(f32) + (total + row_of(mixing_bias)) * valid_rows(
            ends, block * SPAN + core * HALF, HALF
        )
        middle[own(block), :] = center
        unit, _ = norm_parts(center)
        ffn_in[where, :] = (unit * row_of(second_gain) + row_of(second_shift)).astype(bf16)
        attn_share(block).start()


    halves = [slice(n * depth, (n + 1) * depth) for n in range(units // depth)]

    def mask_back(where, start):
        back = (ffn_back[where, :].astype(f32) * valid_rows(ends, start, HALF)).astype(bf16)
        ffn_back[where, :] = back
        collect(0, back.astype(f32))

    def forward(where, columns):
        hidden = dot(ffn_in[where, :], expand_weight[:, columns])
        hidden = hidden + row_of(expand_bias)[:, columns]
        smooth = 0.5 + 0.5 * lax.erf(hidden * (0.5**0.5))
        act[where, columns] = (hidden * smooth).astype(bf16)
        return smooth + hidden * (
            0.3989422804014327 * jnp.exp2(hidden * hidden * (-0.5 * LOG2E))
        )

    def backward(where, number, slope):
        columns = halves[number]
        fresh = (slope * dot(ffn_back[where, :], shrink_weight[columns, :], 1, 1)).astype(bf16)
        hidden_back[where, columns] = fresh
        collect(1 + number, fresh.astype(f32))

    def place(block, theirs):
        start = block * SPAN + (1 - core if theirs else core) * HALF
        return rows(start, HALF), start

    def pass_back(block, theirs):
        where, _ = place(block, theirs)
        part[where, :] = dot(hidden_back[where, :], expand_weight[...], 1, 1).astype(bf16)
        if theirs:
            norm2.to_core(block).start()

    def feed(block, theirs):
        where, start = place(block, theirs)
        mask_back(where, start)
        for number, columns in enumerate(halves):
            backward(where, number, forward(where, columns))
        pass_back(block, theirs)

    def feed_forward(block, theirs):
        where, start = place(block, theirs)
        mask_back(where, start)
        for columns in halves:
            hidden_back[where, columns] = forward(where, columns).astype(bf16)

    def feed_back(block, theirs):
        where, _ = place(block, theirs)
        for number, columns in enumerate(halves):
            backward(where, number, hidden_back[where, columns].astype(f32))
        pass_back(block, theirs)

    def add_out(block):
        def body(where):
            out_part[where, :] = dot(act[where, :], shrink_weight[...]).astype(bf16)

        each_half(block, block + 1, body)
        out.to_core(block).start()

    def norm2_share(block):
        return norm2.share(block, attn_back.at[norm2.ours(block), :], attn_back)

    def finish_norm2(block):
        grad = norm2.result(block)
        unit, rate = norm_parts(middle[own(block), :])
        collect(3, grad * unit)
        collect(4, grad)
        where = norm2.ours(block)
        full = cotangent[block].astype(f32) + norm_back(
            grad, row_of(second_gain), unit, rate
        )
        middle_back[own(block), :] = full
        attn_back[where, :] = (
            full * valid_rows(ends, block * SPAN + core * HALF, HALF)
        ).astype(bf16)
        norm2_share(block).start()


    score_stack = hidden_back
    prob_stack = act
    spare = slice(WINDOW, WINDOW + LANES)
    joined_back = joined

    def turn_back(block):
        where = slice(block * SPAN, (block + 1) * SPAN)
        act[where, spare] = dot(attn_back[where, :], wide_mixing[...], 1, 1).astype(bf16)
        collect(5, attn_back[where, :].astype(f32))

    def attend_back(row_start, count, key_start, keys):
        where = pl.ds(row_start, count)
        key_rows = pl.ds(key_start, keys)
        query = joined[where, 0:LANES]
        back = act[where, spare]
        overlap = back.astype(f32) * context[where, :].astype(f32)
        masks[0:count, 0:keys] = mask_tile(
            ends, seen[:, key_rows], row_start, count, key_start, keys
        )
        query_grad = jnp.zeros((count, LANES), f32)
        step = min(keys, SPAN)
        for head in range(heads):
            mine = head_lanes(head, bf16)
            head_rows = slice(head * count, (head + 1) * count)
            delta = jnp.sum(overlap * head_lanes(head, f32), axis=-1, keepdims=True)
            log_total = log_totals[where, head : head + 1]
            found = jnp.zeros((count, LANES), f32)
            for start in range(0, keys, step):
                chunk = slice(start, start + step)
                chunk_rows = pl.ds(key_start + start, step)
                key = joined[chunk_rows, LANES : 2 * LANES]
                value = joined[chunk_rows, 2 * LANES : 3 * LANES]
                scores = dot(query * mine, key, 1, 1)
                scores = scores * (SCALE * LOG2E) + masks[0:count, chunk]
                probs = jnp.exp2(scores - log_total)
                prob_stack[head_rows, chunk] = probs.astype(bf16)
                change = probs * (dot(back * mine, value, 1, 1) - delta)
                low_change = change.astype(bf16)
                score_stack[head_rows, chunk] = low_change
                found = found + dot(low_change, key)
            query_grad = query_grad + found * head_lanes(head, f32)
        query_low = (query_grad * SCALE).astype(bf16)
        joined_back[where, 0:LANES] = query_low
        collect(6, query_low.astype(f32))
        many_query = jnp.concatenate([query * head_lanes(h, bf16) for h in range(heads)], axis=0)
        many_back = jnp.concatenate([back * head_lanes(h, bf16) for h in range(heads)], axis=0)
        key_grad[key_rows, :] += dot(score_stack[0 : heads * count, 0:keys], many_query, 0, 0)
        value_grad[key_rows, :] += dot(prob_stack[0 : heads * count, 0:keys], many_back, 0, 0)

    def dense_back(first, stop):
        def step(number, carry):
            attend_back(*dense_tile(number))
            return carry

        lax.fori_loop(first, stop, step, 0)

    def each_half(first, stop, body):
        def step(number, carry):
            body(rows(number * HALF, HALF))
            return carry

        lax.fori_loop(2 * first, 2 * stop, step, 0)

    def lower(first, stop):
        def body(where):
            joined_back[where, LANES : 2 * LANES] = (key_grad[where, :] * SCALE).astype(bf16)
            value_low = value_grad[where, :].astype(bf16)
            joined_back[where, 2 * LANES : 3 * LANES] = value_low
            small[6:7, LANES : 2 * LANES] += jnp.sum(
                value_low.astype(f32), axis=0, keepdims=True
            )

        each_half(first, stop, body)

    def project_back(block):
        def body(where):
            part[where, :] = dot(joined_back[where, :], wide_weight[...]).astype(bf16)

        each_half(block, block + 1, body)
        norm1.to_core(block).start()

    def weigh():
        held[last, 0 : 3 * width, :] = jnp.zeros((3 * width, depth), bf16)

        def step(number, carry):
            lanes = rows(number * LANES, LANES)
            wide = dot(joined_back[:, lanes], normed[...], 0, 0).astype(bf16)
            placed = dot(spread_columns(heads, number), wide)
            held[last, 0 : 3 * width, :] = (
                placed + held[last, 0 : 3 * width, :].astype(f32)
            ).astype(bf16)
            return carry

        lax.fori_loop(0, 3, step, 0)

    def input_copies(block):
        source = middle_back.at[own(block), :]
        return (
            norm1.share(block, source, input_grad),
            pltpu.make_async_copy(
                source, input_grad.at[norm1.ours(block), :], input_sems.at[block]
            ),
        )

    def finish_norm1(block):
        grad = norm1.result(block)
        unit, rate = norm_parts(tokens[norm1.ours(block), :].astype(f32))
        collect(7, grad * unit)
        collect(8, grad)
        middle_back[own(block), :] += norm_back(grad, row_of(first_gain), unit, rate)
        for copy in input_copies(block):
            copy.start()

    def output_copies(block):
        where = out.ours(block)
        return (
            out.share(block, ffn_in.at[where, :], layer_output),
            pltpu.make_async_copy(
                ffn_in.at[where, :], layer_output.at[where, :], output_sems.at[block]
            ),
        )

    def finish_out(block):
        total = out.result(block) + row_of(shrink_bias)
        ffn_in[out.ours(block), :] = (
            middle[own(block), :]
            + total * valid_rows(ends, block * SPAN + core * HALF, HALF)
        ).astype(bf16)
        for copy in output_copies(block):
            copy.start()


    steps = height // HALF
    first = WINDOW // HALF - 1
    lax.fori_loop(first, steps, project_step, 0)
    for tile in short_tiles:
        attend(*tile)
    mix(2)
    lax.fori_loop(0, first, project_step, 0)
    attn.cross(2)
    dense(0, 2)
    mix(0)
    dense(2, 3)
    attn.cross(0)
    dense(3, 4)
    mix(1)
    finish_attn(2)
    attn.cross(1)
    for load in loads:
        load.wait()
    attn_share(2).wait()
    feed(2, True)
    feed(2, False)
    finish_attn(0)
    norm2.cross(2)
    attn_share(0).wait()
    feed(0, True)
    feed(0, False)
    finish_attn(1)
    norm2.cross(0)
    attn_share(1).wait()
    feed_forward(1, True)
    feed_forward(1, False)
    for number, columns in enumerate(halves):
        held[number] = dot(act[:, columns], ffn_back[...], 0, 0).astype(bf16)
        begin(number)
    feed_back(1, True)
    feed_back(1, False)
    norm2.cross(1)
    for number, columns in enumerate(halves):
        held[2 + number] = dot(ffn_in[...], hidden_back[:, columns], 0, 0).astype(bf16)
    finish_norm2(2)
    key_grad[...] = jnp.zeros_like(key_grad)
    value_grad[...] = jnp.zeros_like(value_grad)
    norm2_share(2).wait()
    add_out(2)
    add_out(0)
    begin(2)
    add_out(1)
    push(0)
    out.cross(2)
    turn_back(2)
    push(1)
    for tile in short_tiles:
        attend_back(*tile)
    lower(2, 3)
    project_back(2)
    finish_norm2(0)
    out.cross(0)
    begin(3)
    push(0, 2)
    norm2_share(0).wait()
    turn_back(0)
    norm1.cross(2)
    dense_back(0, 2)
    push(2)
    finish_norm2(1)
    push(3, 1, 0)
    norm2_share(1).wait()
    turn_back(1)
    held[last, 3 * width : 4 * width, :] = dot(context[...], attn_back[...], 0, 0)[
        0:width, :
    ].astype(bf16)
    dense_back(2, 3)
    push(2)
    dense_back(3, 4)
    push(1, 0)
    lower(0, 2)
    weigh()
    begin(last)
    push(3)
    project_back(0)
    out.cross(1)
    project_back(1)
    push(2)
    norm1.cross(0)
    push(3, last, 0)
    norm1.cross(1)
    push(1)
    finish_norm1(2)
    push(2)
    push(3, last)
    finish_norm1(0)
    finish_out(2)
    finish_out(0)
    push(last)
    push(3)
    finish_norm1(1)
    push(last)
    small[9:10, :] = jnp.full((1, depth), ends[-1], jnp.int32).astype(f32)
    small_sum[0] = small[...]
    copy = send(small_sum.at[0], small_in.at[0], small_sems, 0, sibling)
    copy.start()
    copy.wait()
    line = lax.broadcasted_iota(jnp.int32, (16, 1), 0)
    both = (line == 3) | (line == 4) | (line == 7) | (line == 8)
    small_sum[1] = small_sum[0] + jnp.where(both, small_in[0], 0.0)
    for level in range(levels):
        copy = pltpu.make_async_remote_copy(
            src_ref=small_sum.at[1 + level],
            dst_ref=small_in.at[1 + level],
            send_sem=small_sems.at[0, 1 + level],
            recv_sem=small_sems.at[1, 1 + level],
            device_id={"dp": partners[level][1]},
            device_id_type=MESH,
        )
        copy.start()
        copy.wait()
        small_sum[2 + level] = small_sum[1 + level] + small_in[1 + level]
    small[...] = small_sum[1 + levels]
    finish_out(1)
    push(1, last, 2, 0, 3, 1, last)
    while not all(merge.finished() for merge in merges):
        push(*range(last + 1))
    for block in range(blocks):
        for copy in input_copies(block) + output_copies(block):
            copy.wait()


def final_kernel(
    heads,
    dp,
    grads,
    small,
    layer_source,
    input_source,
    attend_grad,
    attend_bias_grad,
    mixing_grad,
    mixing_bias_grad,
    expand_grad,
    expand_bias_grad,
    shrink_grad,
    shrink_bias_grad,
    first_gain_grad,
    first_shift_grad,
    second_gain_grad,
    second_shift_grad,
    layer_output,
    input_grad,
    sums,
    stage,
    layer_held,
    input_held,
    load_sems,
    sems,
):
    width = heads * HEAD_DIM
    depth = grads.shape[1]
    factor = dp / small[9:10, :]
    chunks = grads.shape[0]
    last = chunks - 1
    loads = [
        pltpu.make_async_copy(grads.at[number], sums.at[number], load_sems.at[number])
        for number in range(chunks)
    ]
    passes = (
        (layer_source, layer_held, layer_output),
        (input_source, input_held, input_grad),
    )
    for number, (source, middle, _) in enumerate(passes):
        loads.append(pltpu.make_async_copy(source, middle, load_sems.at[chunks + number]))
    for load in loads:
        load.start()
    copies = []
    targets = (
        (0, 0, depth, shrink_grad.at[0:depth, :]),
        (1, 0, depth, shrink_grad.at[depth : 2 * depth, :]),
        (2, 0, depth, expand_grad.at[:, 0:depth]),
        (3, 0, depth, expand_grad.at[:, depth : 2 * depth]),
        (last, 0, 3 * width, attend_grad),
        (last, 3 * width, width, mixing_grad),
    )
    for index, (number, start, count, target) in enumerate(targets):
        if start == 0:
            loads[number].wait()
        stage[number, start : start + count, :] = (
            sums[number, start : start + count, :].astype(f32) * factor
        )
        copy = pltpu.make_async_copy(
            stage.at[number, start : start + count, :], target, sems.at[index]
        )
        copy.start()
        copies.append(copy)
    for number, (_, middle, target) in enumerate(passes):
        loads[chunks + number].wait()
        copy = pltpu.make_async_copy(middle, target, sems.at[6 + number])
        copy.start()
        copies.append(copy)

    def line(number):
        return small[number : number + 1, :] * factor

    for target, number in (
        (shrink_bias_grad, 0),
        (second_gain_grad, 3),
        (second_shift_grad, 4),
        (mixing_bias_grad, 5),
        (first_gain_grad, 7),
        (first_shift_grad, 8),
    ):
        target[...] = line(number).reshape(depth)
    for number in range(2):
        expand_bias_grad[number * depth : (number + 1) * depth] = line(1 + number).reshape(depth)
    both = line(6)
    for head in range(heads):
        for at, lane in ((0, 0), (LANES, HEAD_DIM)):
            first = at + head * HEAD_DIM
            attend_bias_grad[head : head + 1, lane : lane + HEAD_DIM] = both[
                :, first : first + HEAD_DIM
            ]
    for copy in copies:
        copy.wait()


def shape(*dims, kind=bf16):
    return jax.ShapeDtypeStruct(dims, kind)


def params(number):
    return pltpu.CompilerParams(
        collective_id=number, has_side_effects=True, vmem_limit_bytes=255 * 2**18
    )


def sems(blocks):
    return pltpu.SemaphoreType.DMA((2, blocks))


def per_device(
    tokens,
    attend_weight,
    attend_bias,
    mixing_weight,
    mixing_bias,
    expand_weight,
    expand_bias,
    shrink_weight,
    shrink_bias,
    first_gain,
    first_shift,
    second_gain,
    second_shift,
    item_lengths,
    visible,
    cotangent,
):
    height, depth = tokens.shape
    heads = attend_bias.shape[0]
    units = expand_weight.shape[1]
    width = heads * HEAD_DIM
    blocks = height // SPAN
    own = height // 2
    dp = lax.axis_size("dp")
    levels = dp.bit_length() - 1
    chunks = 1 + 2 * units // depth
    low = lambda *dims: pltpu.VMEM(dims, bf16)
    high = lambda *dims: pltpu.VMEM(dims, f32)
    block_buffer = low(blocks, HALF, depth)
    sum_sems = pltpu.SemaphoreType.DMA((2, 3, blocks))

    layer_output, input_grad, grads, small = pl.pallas_call(
        functools.partial(layer_kernel, heads, dp),
        out_shape=(
            shape(height, depth),
            shape(height, depth, kind=f32),
            shape(chunks, depth, depth),
            shape(16, depth, kind=f32),
        ),
        in_specs=[VMEM] * 12 + [SMEM] + [ANY] * 3,
        out_specs=(ANY, ANY, ANY, VMEM),
        scratch_shapes=[
            low(depth, units),
            low(units, depth),
            block_buffer,
            low(height, depth),
            low(height, 3 * LANES),
            low(3 * LANES, depth),
            low(height, LANES),
            high(height, 128),
            high(own, depth),
            high(own, depth),
            low(LANES, depth),
            high(1, 3 * LANES),
            pltpu.VMEM((1, height), jnp.int32),
            high(HALF, WINDOW),
            low(height, depth),
            low(height, units),
            low(height, units),
            low(height, depth),
            low(height, depth),
            high(height, LANES),
            high(height, LANES),
            low(height, depth),
            block_buffer,
            block_buffer,
            block_buffer,
            block_buffer,
            low(HALF, depth),
            low(chunks, depth, depth),
            low(chunks, arrivals(depth, levels), depth),
            high(levels + 2, 16, depth),
            high(levels + 2, 16, depth),
            sum_sems,
            sum_sems,
            sum_sems,
            sum_sems,
            pltpu.SemaphoreType.DMA((2, chunks, 2 * levels)),
            pltpu.SemaphoreType.DMA((chunks,)),
            sems(1 + levels),
            pltpu.SemaphoreType.DMA((3 + blocks,)),
            pltpu.SemaphoreType.DMA((blocks,)),
            pltpu.SemaphoreType.DMA((blocks,)),
        ],
        compiler_params=params(0),
        name="layer",
    )(
        tokens,
        attend_weight.T,
        attend_bias,
        mixing_weight,
        mixing_bias,
        first_gain,
        first_shift,
        second_gain,
        second_shift,
        expand_bias,
        shrink_bias,
        visible,
        item_lengths,
        expand_weight,
        shrink_weight,
        cotangent,
    )

    vector = shape(depth, kind=f32)
    outs = pl.pallas_call(
        functools.partial(final_kernel, heads, dp),
        out_shape=(
            shape(3 * width, depth, kind=f32),
            shape(heads, 2 * HEAD_DIM, kind=f32),
            shape(width, depth, kind=f32),
            vector,
            shape(depth, units, kind=f32),
            shape(units, kind=f32),
            shape(units, depth, kind=f32),
            vector,
            vector,
            vector,
            vector,
            vector,
            shape(height, depth),
            shape(height, depth, kind=f32),
        ),
        in_specs=[ANY, VMEM, ANY, ANY],
        out_specs=(ANY, VMEM, ANY, VMEM, ANY, VMEM, ANY) + (VMEM,) * 5 + (ANY,) * 2,
        scratch_shapes=[
            low(chunks, depth, depth),
            high(chunks, depth, depth),
            low(height, depth),
            high(height, depth),
            pltpu.SemaphoreType.DMA((chunks + 2,)),
            pltpu.SemaphoreType.DMA((8,)),
        ],
        compiler_params=pltpu.CompilerParams(vmem_limit_bytes=60 * 2**20),
        name="final",
    )(grads, small, layer_output, input_grad)
    return (outs[12], outs[13], outs[0].T) + tuple(outs[1:12])


def solution(mesh):
    placed = (
        P("dp", None),
        P(None, "tensor"),
        P("tensor", None),
        P("tensor", None),
        P(),
        P(None, "tensor"),
        P("tensor"),
        P("tensor", None),
        P(),
        P(),
        P(),
        P(),
        P(),
        P("dp", None),
        P("dp"),
        P("dp", None),
    )
    return jax.shard_map(
        per_device,
        mesh=mesh,
        in_specs=placed,
        out_specs=(
            P("dp", None),
            P("dp", None),
            P(None, "tensor"),
            P("tensor", None),
            P("tensor", None),
            P(),
            P(None, "tensor"),
            P("tensor"),
            P("tensor", None),
            P(),
            P(),
            P(),
            P(),
            P(),
        ),
        check_vma=False,
    )
```

```python
import functools

import jax
import jax.numpy as jnp
from jax import lax
from jax.experimental import pallas as pl
from jax.experimental.pallas import tpu as pltpu
from jax.sharding import PartitionSpec as P

HEAD_DIM = 32
LANES = 256
SPAN = 512
HALF = SPAN // 2
WINDOW = 1024
EPS = 1e-05
LOG2E = 1.4426950408889634
MASKED = -1e30
MESH = pl.DeviceIdType.MESH
f32 = jnp.float32
bf16 = jnp.bfloat16
VMEM = pl.BlockSpec(memory_space=pltpu.VMEM)
ANY = pl.BlockSpec(memory_space=pl.ANY)
SMEM = pl.BlockSpec(memory_space=pltpu.SMEM)


def dot(left, right, left_dim=1, right_dim=0):
    return lax.dot_general(
        left, right, (((left_dim,), (right_dim,)), ((), ())), preferred_element_type=f32
    )


def norm_parts(values):
    center = values - jnp.mean(values, axis=-1, keepdims=True)
    spread = jnp.mean(center * center, axis=-1, keepdims=True)
    rate = lax.rsqrt(spread + EPS)
    return center * rate, rate


def norm_back(grad, gain, unit, rate):
    scaled = grad * gain
    first = jnp.mean(scaled, axis=-1, keepdims=True)
    second = jnp.mean(scaled * unit, axis=-1, keepdims=True)
    return rate * (scaled - first - unit * second)


def neighbours():
    place = lax.axis_index("tensor")
    core = place % 2
    chip = place // 2
    return core, chip * 2 + (1 - core), (1 - chip) * 2 + core


def greet(sibling, across, partners=()):
    barrier = pltpu.get_barrier_semaphore()
    for other in (sibling, across):
        pl.semaphore_signal(barrier, inc=1, device_id={"tensor": other}, device_id_type=MESH)
    for other in partners:
        pl.semaphore_signal(barrier, inc=1, device_id={"dp": other}, device_id_type=MESH)
    pl.semaphore_wait(barrier, 2 + len(partners))


def send(source, target, sems, slot, other):
    return pltpu.make_async_remote_copy(
        src_ref=source,
        dst_ref=target,
        send_sem=sems.at[0, slot],
        recv_sem=sems.at[1, slot],
        device_id={"tensor": other},
        device_id_type=MESH,
    )


def row_of(vector):
    return vector[...].reshape(1, vector.shape[0])


def dp_partners(size):
    place = lax.axis_index("dp")
    found = []
    step = 1
    while step < size:
        bit = (place // step) % 2
        found.append((bit, place + (1 - 2 * bit) * step))
        step *= 2
    return found


def halving(length, levels):
    plan = []
    for _ in range(levels):
        halve = (length // 2) % 16 == 0
        plan.append((length, halve))
        length = length // 2 if halve else length
    return plan


def arrivals(length, levels):
    return sum(held // 2 if halve else held for held, halve in halving(length, levels))


class Merge:
    def __init__(self, held, final, arrived, sems, keep_sems, slot, partners, order):
        self.held, self.final, self.arrived = held, final, arrived
        self.sems, self.keep_sems = sems, keep_sems
        self.slot = slot
        self.done = 0
        self.kept = False
        self.steps = []
        length = held.shape[1]
        offset = 0
        place = 0
        for (count, halve), level in zip(halving(length, len(partners)), order):
            bit, partner = partners[level]
            part = count // 2 if halve else count
            keep = offset + bit * part if halve else offset
            give = offset + (1 - bit) * part if halve else offset
            self.steps.append((halve, part, keep, give, place, partner))
            offset = keep
            place += part
        self.last = part

    def where(self, start, count):
        return pl.ds(pl.multiple_of(start, 16), count)

    def own_copy(self):
        where = self.where(self.steps[-1][2], self.last)
        return pltpu.make_async_copy(
            self.held.at[self.slot, where, :],
            self.final.at[self.slot, where, :],
            self.keep_sems.at[self.slot],
        )

    def copy(self, number):
        levels = len(self.steps)
        back = number >= levels
        halve, part, keep, give, place, partner = self.steps[
            2 * levels - 1 - number if back else number
        ]
        if back:
            if not halve:
                return None
            where = self.where(keep, part)
            source = (self.held if part == self.last else self.final).at[self.slot, where, :]
            target = self.final.at[self.slot, where, :]
        else:
            source = self.held.at[self.slot, self.where(give, part), :]
            target = self.arrived.at[self.slot, pl.ds(place, part), :]
        return pltpu.make_async_remote_copy(
            src_ref=source,
            dst_ref=target,
            send_sem=self.sems.at[0, self.slot, number],
            recv_sem=self.sems.at[1, self.slot, number],
            device_id={"dp": partner},
            device_id_type=MESH,
        )

    def start(self):
        copy = self.copy(self.done)
        if copy is not None:
            copy.start()

    def finished(self):
        return self.done == 2 * len(self.steps)

    def advance(self):
        levels = len(self.steps)
        if self.finished():
            return
        number = self.done
        copy = self.copy(number)
        if copy is not None:
            copy.wait()
        if number < levels:
            _, part, keep, _, place, _ = self.steps[number]
            mine = self.where(keep, part)
            self.held[self.slot, mine, :] = (
                self.held[self.slot, mine, :].astype(f32)
                + self.arrived[self.slot, pl.ds(place, part), :].astype(f32)
            ).astype(bf16)
            if number == levels - 1:
                self.own_copy().start()
        elif copy is not None and not self.kept:
            self.own_copy().wait()
            self.kept = True
        self.done += 1
        if not self.finished():
            self.start()


def rows(start, count):
    return pl.ds(pl.multiple_of(start, count), count)


def item_ends(lengths_ref):
    ends = []
    total = 0
    for slot in range(lengths_ref.shape[1]):
        total = total + lengths_ref[0, slot]
        ends.append(total)
    return ends


def item_at(place, ends):
    item = jnp.zeros(place.shape, jnp.int32)
    for end in ends:
        item = item + (place >= end).astype(jnp.int32)
    return item


def mask_tile(ends, visible, row_start, count, key_start, keys):
    row = row_start + lax.broadcasted_iota(jnp.int32, (count, 1), 0)
    key = key_start + lax.broadcasted_iota(jnp.int32, (1, keys), 1)
    allowed = (item_at(row, ends) == item_at(key, ends)) & ((visible == 1) | (row == key))
    return jnp.where(allowed, 0.0, MASKED).astype(f32)


def head_lanes(head, kind):
    lane = lax.broadcasted_iota(jnp.int32, (1, LANES), 1)
    return ((lane >= head * HEAD_DIM) & (lane < (head + 1) * HEAD_DIM)).astype(f32).astype(kind)


def spread_columns(heads, part):
    source = lax.broadcasted_iota(jnp.int32, (heads * 3 * HEAD_DIM, 1), 0)
    inside = lax.broadcasted_iota(jnp.int32, (1, LANES), 1)
    wanted = (inside // HEAD_DIM) * (3 * HEAD_DIM) + part * HEAD_DIM + inside % HEAD_DIM
    wanted = jnp.where(inside < heads * HEAD_DIM, wanted, -1)
    return (source == wanted).astype(f32).astype(bf16)


def valid_rows(ends, start, count):
    row = start + lax.broadcasted_iota(jnp.int32, (count, 1), 0)
    return (row < ends[-1]).astype(f32)


SCALE = HEAD_DIM ** (-0.5)


class Sum:
    def __init__(self, part, from_core, chip_sum, from_chip, sems, core, sibling, across):
        self.part, self.from_core, self.chip_sum, self.from_chip = (
            part,
            from_core,
            chip_sum,
            from_chip,
        )
        self.sems = sems
        self.core, self.sibling, self.across = core, sibling, across

    def ours(self, block):
        return rows(block * SPAN + self.core * HALF, HALF)

    def theirs(self, block):
        return rows(block * SPAN + (1 - self.core) * HALF, HALF)

    def copy(self, source, target, stage, block, other):
        return pltpu.make_async_remote_copy(
            src_ref=source,
            dst_ref=target,
            send_sem=self.sems.at[0, stage, block],
            recv_sem=self.sems.at[1, stage, block],
            device_id={"tensor": other},
            device_id_type=MESH,
        )

    def to_core(self, block):
        return self.copy(
            self.part.at[self.theirs(block), :], self.from_core(block), 0, block, self.sibling
        )

    def to_chip(self, block):
        return self.copy(
            self.chip_sum(block), self.from_chip(block), 1, block, self.across
        )

    def share(self, block, source, target):
        return self.copy(source, target.at[self.ours(block), :], 2, block, self.sibling)

    def cross(self, block):
        self.to_core(block).wait()
        mine = self.part[self.ours(block), :].astype(f32)
        self.chip_sum(block)[...] = (mine + self.from_core(block)[...].astype(f32)).astype(bf16)
        self.to_chip(block).start()

    def result(self, block):
        self.to_chip(block).wait()
        return self.chip_sum(block)[...].astype(f32) + self.from_chip(block)[...].astype(f32)


def merge_order(number, levels):
    near = list(range(levels))
    return near[1:] + near[:1] if number == 1 else near


def layer_kernel(
    heads,
    dp,
    tokens,
    attend_weight,
    attend_bias,
    mixing_weight,
    mixing_bias,
    first_gain,
    first_shift,
    second_gain,
    second_shift,
    expand_bias,
    shrink_bias,
    visible,
    lengths,
    expand_source,
    shrink_source,
    cotangent_source,
    layer_output,
    input_grad,
    grads,
    small,
    expand_weight,
    shrink_weight,
    cotangent,
    normed,
    joined,
    wide_weight,
    context,
    log_totals,
    middle,
    middle_back,
    wide_mixing,
    bias,
    seen,
    masks,
    ffn_in,
    act,
    hidden_back,
    ffn_back,
    attn_back,
    key_grad,
    value_grad,
    part,
    from_core,
    chip_sum,
    from_chip,
    norm2_from_chip,
    norm1_from_chip,
    held,
    arrived,
    small_sum,
    small_in,
    attn_sems,
    norm2_sems,
    norm1_sems,
    out_sems,
    merge_sems,
    keep_sems,
    small_sems,
    load_sems,
    output_sems,
    input_sems,
):
    core, sibling, across = neighbours()
    partners = dp_partners(dp)
    levels = len(partners)
    height, depth = tokens.shape
    units = expand_weight.shape[1]
    blocks = height // SPAN
    width = heads * HEAD_DIM
    last = grads.shape[0] - 1
    ends = item_ends(lengths)
    load_pairs = [
        (expand_source, expand_weight),
        (shrink_source, shrink_weight),
        (cotangent_source, ffn_back),
    ]
    for block in range(blocks):
        mine = rows(block * SPAN + core * HALF, HALF)
        load_pairs.append((cotangent_source.at[mine, :], cotangent.at[block]))
    loads = [
        pltpu.make_async_copy(source, target, load_sems.at[number])
        for number, (source, target) in enumerate(load_pairs)
    ]
    for load in loads:
        load.start()
    greet(sibling, across, [partner for _, partner in partners])
    place3 = (core, sibling, across)
    from_core_at = lambda block: from_core.at[block]
    chip_sum_at = lambda block: chip_sum.at[block]

    def late_from_core(block):
        buffer = act if block == 1 else hidden_back
        lanes = slice(depth, 2 * depth) if block == 2 else slice(0, depth)
        return buffer.at[heads * HALF : heads * HALF + HALF, lanes]

    def late_chip_sum(block):
        return ffn_in.at[rows(block * SPAN + (1 - core) * HALF, HALF), :]

    from_chip_at = lambda block: from_chip.at[block]
    norm2_from_chip_at = lambda block: norm2_from_chip.at[block]

    def late_from_chip(block):
        if block == 2:
            return norm1_from_chip.at[...]
        return expand_weight.at[0:HALF, block * depth : (block + 1) * depth]

    attn = Sum(part, from_core_at, chip_sum_at, from_chip_at, attn_sems, *place3)
    norm2 = Sum(part, from_core_at, chip_sum_at, norm2_from_chip_at, norm2_sems, *place3)
    norm1 = Sum(part, late_from_core, late_chip_sum, late_from_chip, norm1_sems, *place3)
    out_part = ffn_back
    out = Sum(out_part, from_core_at, chip_sum_at, from_chip_at, out_sems, *place3)
    merges = [
        Merge(
            held,
            grads,
            arrived,
            merge_sems,
            keep_sems,
            number,
            partners,
            merge_order(number, levels),
        )
        for number in range(last + 1)
    ]

    def begin(number):
        merges[number].start()

    def push(*numbers):
        for number in numbers:
            merges[number].advance()

    def own(block):
        return slice(block * HALF, (block + 1) * HALF)


    for number in range(3):
        lanes = slice(number * LANES, (number + 1) * LANES)
        wide_weight[lanes, :] = dot(
            spread_columns(heads, number), attend_weight[...], 0, 0
        ).astype(bf16)
    seen[...] = row_of(visible)
    blank = jnp.zeros((1, LANES - width), f32)
    for part_at, lane_at in ((0, 0), (2, HEAD_DIM)):
        pieces = [attend_bias[h : h + 1, lane_at : lane_at + HEAD_DIM] for h in range(heads)]
        bias[:, part_at * LANES : (part_at + 1) * LANES] = jnp.concatenate(
            pieces + [blank], axis=1
        )
    bias[:, LANES : 2 * LANES] = jnp.zeros((1, LANES), f32)
    wide_mixing[...] = jnp.zeros_like(wide_mixing)
    wide_mixing[0:width, :] = mixing_weight[...]
    small[...] = jnp.zeros_like(small)

    def collect(number, values):
        small[number : number + 1, 0 : values.shape[1]] += jnp.sum(values, axis=0, keepdims=True)

    def project_step(step, carry):
        where = rows(step * HALF, HALF)
        unit, _ = norm_parts(tokens[where, :].astype(f32))
        fresh = (unit * row_of(first_gain) + row_of(first_shift)).astype(bf16)
        normed[where, :] = fresh
        joined[where, :] = (dot(fresh, wide_weight[...], 1, 1) + bias[...]).astype(bf16)
        return carry


    short_tiles = [
        (start, 128, min(start - 64, height - 256), 256) for start in range(WINDOW, height, 128)
    ]

    def dense_tile(step):
        return (pl.multiple_of(step * HALF, HALF), HALF, 0, WINDOW)

    def attend(row_start, count, key_start, keys):
        query = joined[pl.ds(row_start, count), 0:LANES]
        key_rows = pl.ds(key_start, keys)
        key = joined[key_rows, LANES : 2 * LANES]
        value = joined[key_rows, 2 * LANES : 3 * LANES]
        masks[0:count, 0:keys] = mask_tile(
            ends, seen[:, key_rows], row_start, count, key_start, keys
        )
        lane = lax.broadcasted_iota(jnp.int32, (1, 128), 1)
        mixed = jnp.zeros((count, LANES), f32)
        stats = jnp.zeros((count, 128), f32)
        for head in range(heads):
            scores = dot(query * head_lanes(head, bf16), key, 1, 1)
            scores = scores * (SCALE * LOG2E) + masks[0:count, 0:keys]
            top = jnp.max(scores, axis=-1, keepdims=True)
            powers = jnp.exp2(scores - top)
            total = jnp.sum(powers, axis=-1, keepdims=True)
            mine = dot(powers.astype(bf16), value) / total
            mixed = mixed + mine * head_lanes(head, f32)
            stats = jnp.where(lane == head, top + jnp.log2(total), stats)
        context[pl.ds(row_start, count), :] = mixed.astype(bf16)
        log_totals[pl.ds(row_start, count), :] = stats

    def dense(first, stop):
        def step(number, carry):
            attend(*dense_tile(number))
            return carry

        lax.fori_loop(first, stop, step, 0)

    def mix(block):
        def body(where):
            part[where, :] = dot(context[where, :], wide_mixing[...]).astype(bf16)

        each_half(block, block + 1, body)
        attn.to_core(block).start()

    def attn_share(block):
        where = attn.ours(block)
        return attn.share(block, ffn_in.at[where, :], ffn_in)

    def finish_attn(block):
        total = attn.result(block)
        where = attn.ours(block)
        center = tokens[where, :].astype(f32) + (total + row_of(mixing_bias)) * valid_rows(
            ends, block * SPAN + core * HALF, HALF
        )
        middle[own(block), :] = center
        unit, _ = norm_parts(center)
        ffn_in[where, :] = (unit * row_of(second_gain) + row_of(second_shift)).astype(bf16)
        attn_share(block).start()


    halves = [slice(n * depth, (n + 1) * depth) for n in range(units // depth)]

    def mask_back(where, start):
        back = (ffn_back[where, :].astype(f32) * valid_rows(ends, start, HALF)).astype(bf16)
        ffn_back[where, :] = back
        collect(0, back.astype(f32))

    def forward(where, columns):
        hidden = dot(ffn_in[where, :], expand_weight[:, columns])
        hidden = hidden + row_of(expand_bias)[:, columns]
        smooth = 0.5 + 0.5 * lax.erf(hidden * (0.5**0.5))
        act[where, columns] = (hidden * smooth).astype(bf16)
        return smooth + hidden * (
            0.3989422804014327 * jnp.exp2(hidden * hidden * (-0.5 * LOG2E))
        )

    def backward(where, number, slope):
        columns = halves[number]
        fresh = (slope * dot(ffn_back[where, :], shrink_weight[columns, :], 1, 1)).astype(bf16)
        hidden_back[where, columns] = fresh
        collect(1 + number, fresh.astype(f32))

    def place(block, theirs):
        start = block * SPAN + (1 - core if theirs else core) * HALF
        return rows(start, HALF), start

    def pass_back(block, theirs):
        where, _ = place(block, theirs)
        part[where, :] = dot(hidden_back[where, :], expand_weight[...], 1, 1).astype(bf16)
        if theirs:
            norm2.to_core(block).start()

    def feed(block, theirs):
        where, start = place(block, theirs)
        mask_back(where, start)
        for number, columns in enumerate(halves):
            backward(where, number, forward(where, columns))
        pass_back(block, theirs)

    def feed_forward(block, theirs):
        where, start = place(block, theirs)
        mask_back(where, start)
        for columns in halves:
            hidden_back[where, columns] = forward(where, columns).astype(bf16)

    def feed_back(block, theirs):
        where, _ = place(block, theirs)
        for number, columns in enumerate(halves):
            backward(where, number, hidden_back[where, columns].astype(f32))
        pass_back(block, theirs)

    def add_out(block):
        def body(where):
            out_part[where, :] = dot(act[where, :], shrink_weight[...]).astype(bf16)

        each_half(block, block + 1, body)
        out.to_core(block).start()

    def norm2_share(block):
        return norm2.share(block, attn_back.at[norm2.ours(block), :], attn_back)

    def finish_norm2(block):
        grad = norm2.result(block)
        unit, rate = norm_parts(middle[own(block), :])
        collect(3, grad * unit)
        collect(4, grad)
        where = norm2.ours(block)
        full = cotangent[block].astype(f32) + norm_back(
            grad, row_of(second_gain), unit, rate
        )
        middle_back[own(block), :] = full
        attn_back[where, :] = (
            full * valid_rows(ends, block * SPAN + core * HALF, HALF)
        ).astype(bf16)
        norm2_share(block).start()


    score_stack = hidden_back
    prob_stack = act
    spare = slice(WINDOW, WINDOW + LANES)
    joined_back = joined

    def turn_back(block):
        where = slice(block * SPAN, (block + 1) * SPAN)
        act[where, spare] = dot(attn_back[where, :], wide_mixing[...], 1, 1).astype(bf16)
        collect(5, attn_back[where, :].astype(f32))

    def attend_back(row_start, count, key_start, keys):
        where = pl.ds(row_start, count)
        key_rows = pl.ds(key_start, keys)
        query = joined[where, 0:LANES]
        back = act[where, spare]
        overlap = back.astype(f32) * context[where, :].astype(f32)
        masks[0:count, 0:keys] = mask_tile(
            ends, seen[:, key_rows], row_start, count, key_start, keys
        )
        query_grad = jnp.zeros((count, LANES), f32)
        step = min(keys, SPAN)
        for head in range(heads):
            mine = head_lanes(head, bf16)
            head_rows = slice(head * count, (head + 1) * count)
            delta = jnp.sum(overlap * head_lanes(head, f32), axis=-1, keepdims=True)
            log_total = log_totals[where, head : head + 1]
            found = jnp.zeros((count, LANES), f32)
            for start in range(0, keys, step):
                chunk = slice(start, start + step)
                chunk_rows = pl.ds(key_start + start, step)
                key = joined[chunk_rows, LANES : 2 * LANES]
                value = joined[chunk_rows, 2 * LANES : 3 * LANES]
                scores = dot(query * mine, key, 1, 1)
                scores = scores * (SCALE * LOG2E) + masks[0:count, chunk]
                probs = jnp.exp2(scores - log_total)
                prob_stack[head_rows, chunk] = probs.astype(bf16)
                change = probs * (dot(back * mine, value, 1, 1) - delta)
                low_change = change.astype(bf16)
                score_stack[head_rows, chunk] = low_change
                found = found + dot(low_change, key)
            query_grad = query_grad + found * head_lanes(head, f32)
        query_low = (query_grad * SCALE).astype(bf16)
        joined_back[where, 0:LANES] = query_low
        collect(6, query_low.astype(f32))
        many_query = jnp.concatenate([query * head_lanes(h, bf16) for h in range(heads)], axis=0)
        many_back = jnp.concatenate([back * head_lanes(h, bf16) for h in range(heads)], axis=0)
        key_grad[key_rows, :] += dot(score_stack[0 : heads * count, 0:keys], many_query, 0, 0)
        value_grad[key_rows, :] += dot(prob_stack[0 : heads * count, 0:keys], many_back, 0, 0)

    def dense_back(first, stop):
        def step(number, carry):
            attend_back(*dense_tile(number))
            return carry

        lax.fori_loop(first, stop, step, 0)

    def each_half(first, stop, body):
        def step(number, carry):
            body(rows(number * HALF, HALF))
            return carry

        lax.fori_loop(2 * first, 2 * stop, step, 0)

    def lower(first, stop):
        def body(where):
            joined_back[where, LANES : 2 * LANES] = (key_grad[where, :] * SCALE).astype(bf16)
            value_low = value_grad[where, :].astype(bf16)
            joined_back[where, 2 * LANES : 3 * LANES] = value_low
            small[6:7, LANES : 2 * LANES] += jnp.sum(
                value_low.astype(f32), axis=0, keepdims=True
            )

        each_half(first, stop, body)

    def project_back(block):
        def body(where):
            part[where, :] = dot(joined_back[where, :], wide_weight[...]).astype(bf16)

        each_half(block, block + 1, body)
        norm1.to_core(block).start()

    def weigh():
        held[last, 0 : 3 * width, :] = jnp.zeros((3 * width, depth), bf16)

        def step(number, carry):
            lanes = rows(number * LANES, LANES)
            wide = dot(joined_back[:, lanes], normed[...], 0, 0).astype(bf16)
            placed = dot(spread_columns(heads, number), wide)
            held[last, 0 : 3 * width, :] = (
                placed + held[last, 0 : 3 * width, :].astype(f32)
            ).astype(bf16)
            return carry

        lax.fori_loop(0, 3, step, 0)

    def input_copies(block):
        source = middle_back.at[own(block), :]
        return (
            norm1.share(block, source, input_grad),
            pltpu.make_async_copy(
                source, input_grad.at[norm1.ours(block), :], input_sems.at[block]
            ),
        )

    def finish_norm1(block):
        grad = norm1.result(block)
        unit, rate = norm_parts(tokens[norm1.ours(block), :].astype(f32))
        collect(7, grad * unit)
        collect(8, grad)
        middle_back[own(block), :] += norm_back(grad, row_of(first_gain), unit, rate)
        for copy in input_copies(block):
            copy.start()

    def output_copies(block):
        where = out.ours(block)
        return (
            out.share(block, ffn_in.at[where, :], layer_output),
            pltpu.make_async_copy(
                ffn_in.at[where, :], layer_output.at[where, :], output_sems.at[block]
            ),
        )

    def finish_out(block):
        total = out.result(block) + row_of(shrink_bias)
        ffn_in[out.ours(block), :] = (
            middle[own(block), :]
            + total * valid_rows(ends, block * SPAN + core * HALF, HALF)
        ).astype(bf16)
        for copy in output_copies(block):
            copy.start()


    steps = height // HALF
    first = WINDOW // HALF - 1
    lax.fori_loop(first, steps, project_step, 0)
    for tile in short_tiles:
        attend(*tile)
    mix(2)
    lax.fori_loop(0, first, project_step, 0)
    attn.cross(2)
    dense(0, 2)
    mix(0)
    dense(2, 3)
    attn.cross(0)
    dense(3, 4)
    mix(1)
    finish_attn(2)
    attn.cross(1)
    for load in loads:
        load.wait()
    attn_share(2).wait()
    feed(2, True)
    feed(2, False)
    finish_attn(0)
    norm2.cross(2)
    attn_share(0).wait()
    feed(0, True)
    feed(0, False)
    finish_attn(1)
    norm2.cross(0)
    attn_share(1).wait()
    feed_forward(1, True)
    feed_forward(1, False)
    for number, columns in enumerate(halves):
        held[number] = dot(act[:, columns], ffn_back[...], 0, 0).astype(bf16)
        begin(number)
    feed_back(1, True)
    feed_back(1, False)
    norm2.cross(1)
    for number, columns in enumerate(halves):
        held[2 + number] = dot(ffn_in[...], hidden_back[:, columns], 0, 0).astype(bf16)
    finish_norm2(2)
    key_grad[...] = jnp.zeros_like(key_grad)
    value_grad[...] = jnp.zeros_like(value_grad)
    norm2_share(2).wait()
    add_out(2)
    add_out(0)
    begin(2)
    add_out(1)
    push(0)
    out.cross(2)
    turn_back(2)
    push(1)
    for tile in short_tiles:
        attend_back(*tile)
    lower(2, 3)
    project_back(2)
    finish_norm2(0)
    out.cross(0)
    begin(3)
    push(0, 2)
    norm2_share(0).wait()
    turn_back(0)
    norm1.cross(2)
    dense_back(0, 1)
    push(2)
    dense_back(1, 2)
    push(2)
    finish_norm2(1)
    push(3, 1, 0)
    norm2_share(1).wait()
    turn_back(1)
    held[last, 3 * width : 4 * width, :] = dot(context[...], attn_back[...], 0, 0)[
        0:width, :
    ].astype(bf16)
    dense_back(2, 3)
    push(2, 3)
    dense_back(3, 4)
    push(1, 0)
    lower(0, 2)
    weigh()
    begin(last)
    push(3)
    project_back(0)
    out.cross(1)
    project_back(1)
    push(2)
    norm1.cross(0)
    push(3, last, 0)
    norm1.cross(1)
    push(1)
    finish_norm1(2)
    push(2)
    push(3, last)
    finish_norm1(0)
    finish_out(2)
    finish_out(0)
    push(last)
    push(3)
    finish_norm1(1)
    push(last)
    small[9:10, :] = jnp.full((1, depth), ends[-1], jnp.int32).astype(f32)
    small_sum[0] = small[...]
    copy = send(small_sum.at[0], small_in.at[0], small_sems, 0, sibling)
    copy.start()
    copy.wait()
    line = lax.broadcasted_iota(jnp.int32, (16, 1), 0)
    both = (line == 3) | (line == 4) | (line == 7) | (line == 8)
    small_sum[1] = small_sum[0] + jnp.where(both, small_in[0], 0.0)
    for level in range(levels):
        copy = pltpu.make_async_remote_copy(
            src_ref=small_sum.at[1 + level],
            dst_ref=small_in.at[1 + level],
            send_sem=small_sems.at[0, 1 + level],
            recv_sem=small_sems.at[1, 1 + level],
            device_id={"dp": partners[level][1]},
            device_id_type=MESH,
        )
        copy.start()
        push((1, last, 2, 0, 3)[level % 5])
        copy.wait()
        small_sum[2 + level] = small_sum[1 + level] + small_in[1 + level]
    small[...] = small_sum[1 + levels]
    finish_out(1)
    push(0, 3, 1, last)
    while not all(merge.finished() for merge in merges):
        push(*range(last + 1))
    for block in range(blocks):
        for copy in input_copies(block) + output_copies(block):
            copy.wait()


def final_kernel(
    heads,
    dp,
    grads,
    small,
    layer_source,
    input_source,
    attend_grad,
    attend_bias_grad,
    mixing_grad,
    mixing_bias_grad,
    expand_grad,
    expand_bias_grad,
    shrink_grad,
    shrink_bias_grad,
    first_gain_grad,
    first_shift_grad,
    second_gain_grad,
    second_shift_grad,
    layer_output,
    input_grad,
    sums,
    stage,
    layer_held,
    input_held,
    load_sems,
    sems,
):
    width = heads * HEAD_DIM
    depth = grads.shape[1]
    factor = dp / small[9:10, :]
    chunks = grads.shape[0]
    last = chunks - 1
    loads = [
        pltpu.make_async_copy(grads.at[number], sums.at[number], load_sems.at[number])
        for number in range(chunks)
    ]
    passes = (
        (layer_source, layer_held, layer_output),
        (input_source, input_held, input_grad),
    )
    for number, (source, middle, _) in enumerate(passes):
        loads.append(pltpu.make_async_copy(source, middle, load_sems.at[chunks + number]))
    for load in loads:
        load.start()
    copies = []
    targets = (
        (0, 0, depth, shrink_grad.at[0:depth, :]),
        (1, 0, depth, shrink_grad.at[depth : 2 * depth, :]),
        (2, 0, depth, expand_grad.at[:, 0:depth]),
        (3, 0, depth, expand_grad.at[:, depth : 2 * depth]),
        (last, 0, 3 * width, attend_grad),
        (last, 3 * width, width, mixing_grad),
    )
    for index, (number, start, count, target) in enumerate(targets):
        if start == 0:
            loads[number].wait()
        stage[number, start : start + count, :] = (
            sums[number, start : start + count, :].astype(f32) * factor
        )
        copy = pltpu.make_async_copy(
            stage.at[number, start : start + count, :], target, sems.at[index]
        )
        copy.start()
        copies.append(copy)
    for number, (_, middle, target) in enumerate(passes):
        loads[chunks + number].wait()
        copy = pltpu.make_async_copy(middle, target, sems.at[6 + number])
        copy.start()
        copies.append(copy)

    def line(number):
        return small[number : number + 1, :] * factor

    for target, number in (
        (shrink_bias_grad, 0),
        (second_gain_grad, 3),
        (second_shift_grad, 4),
        (mixing_bias_grad, 5),
        (first_gain_grad, 7),
        (first_shift_grad, 8),
    ):
        target[...] = line(number).reshape(depth)
    for number in range(2):
        expand_bias_grad[number * depth : (number + 1) * depth] = line(1 + number).reshape(depth)
    both = line(6)
    for head in range(heads):
        for at, lane in ((0, 0), (LANES, HEAD_DIM)):
            first = at + head * HEAD_DIM
            attend_bias_grad[head : head + 1, lane : lane + HEAD_DIM] = both[
                :, first : first + HEAD_DIM
            ]
    for copy in copies:
        copy.wait()


def shape(*dims, kind=bf16):
    return jax.ShapeDtypeStruct(dims, kind)


def params(number):
    return pltpu.CompilerParams(
        collective_id=number, has_side_effects=True, vmem_limit_bytes=255 * 2**18
    )


def sems(blocks):
    return pltpu.SemaphoreType.DMA((2, blocks))


def per_device(
    tokens,
    attend_weight,
    attend_bias,
    mixing_weight,
    mixing_bias,
    expand_weight,
    expand_bias,
    shrink_weight,
    shrink_bias,
    first_gain,
    first_shift,
    second_gain,
    second_shift,
    item_lengths,
    visible,
    cotangent,
):
    height, depth = tokens.shape
    heads = attend_bias.shape[0]
    units = expand_weight.shape[1]
    width = heads * HEAD_DIM
    blocks = height // SPAN
    own = height // 2
    dp = lax.axis_size("dp")
    levels = dp.bit_length() - 1
    chunks = 1 + 2 * units // depth
    low = lambda *dims: pltpu.VMEM(dims, bf16)
    high = lambda *dims: pltpu.VMEM(dims, f32)
    block_buffer = low(blocks, HALF, depth)
    sum_sems = pltpu.SemaphoreType.DMA((2, 3, blocks))

    layer_output, input_grad, grads, small = pl.pallas_call(
        functools.partial(layer_kernel, heads, dp),
        out_shape=(
            shape(height, depth),
            shape(height, depth, kind=f32),
            shape(chunks, depth, depth),
            shape(16, depth, kind=f32),
        ),
        in_specs=[VMEM] * 12 + [SMEM] + [ANY] * 3,
        out_specs=(ANY, ANY, ANY, VMEM),
        scratch_shapes=[
            low(depth, units),
            low(units, depth),
            block_buffer,
            low(height, depth),
            low(height, 3 * LANES),
            low(3 * LANES, depth),
            low(height, LANES),
            high(height, 128),
            high(own, depth),
            high(own, depth),
            low(LANES, depth),
            high(1, 3 * LANES),
            pltpu.VMEM((1, height), jnp.int32),
            high(HALF, WINDOW),
            low(height, depth),
            low(height, units),
            low(height, units),
            low(height, depth),
            low(height, depth),
            high(height, LANES),
            high(height, LANES),
            low(height, depth),
            block_buffer,
            block_buffer,
            block_buffer,
            block_buffer,
            low(HALF, depth),
            low(chunks, depth, depth),
            low(chunks, arrivals(depth, levels), depth),
            high(levels + 2, 16, depth),
            high(levels + 2, 16, depth),
            sum_sems,
            sum_sems,
            sum_sems,
            sum_sems,
            pltpu.SemaphoreType.DMA((2, chunks, 2 * levels)),
            pltpu.SemaphoreType.DMA((chunks,)),
            sems(1 + levels),
            pltpu.SemaphoreType.DMA((3 + blocks,)),
            pltpu.SemaphoreType.DMA((blocks,)),
            pltpu.SemaphoreType.DMA((blocks,)),
        ],
        compiler_params=params(0),
        name="layer",
    )(
        tokens,
        attend_weight.T,
        attend_bias,
        mixing_weight,
        mixing_bias,
        first_gain,
        first_shift,
        second_gain,
        second_shift,
        expand_bias,
        shrink_bias,
        visible,
        item_lengths,
        expand_weight,
        shrink_weight,
        cotangent,
    )

    vector = shape(depth, kind=f32)
    outs = pl.pallas_call(
        functools.partial(final_kernel, heads, dp),
        out_shape=(
            shape(3 * width, depth, kind=f32),
            shape(heads, 2 * HEAD_DIM, kind=f32),
            shape(width, depth, kind=f32),
            vector,
            shape(depth, units, kind=f32),
            shape(units, kind=f32),
            shape(units, depth, kind=f32),
            vector,
            vector,
            vector,
            vector,
            vector,
            shape(height, depth),
            shape(height, depth, kind=f32),
        ),
        in_specs=[ANY, VMEM, ANY, ANY],
        out_specs=(ANY, VMEM, ANY, VMEM, ANY, VMEM, ANY) + (VMEM,) * 5 + (ANY,) * 2,
        scratch_shapes=[
            low(chunks, depth, depth),
            high(chunks, depth, depth),
            low(height, depth),
            high(height, depth),
            pltpu.SemaphoreType.DMA((chunks + 2,)),
            pltpu.SemaphoreType.DMA((8,)),
        ],
        compiler_params=pltpu.CompilerParams(vmem_limit_bytes=60 * 2**20),
        name="final",
    )(grads, small, layer_output, input_grad)
    return (outs[12], outs[13], outs[0].T) + tuple(outs[1:12])


def solution(mesh):
    placed = (
        P("dp", None),
        P(None, "tensor"),
        P("tensor", None),
        P("tensor", None),
        P(),
        P(None, "tensor"),
        P("tensor"),
        P("tensor", None),
        P(),
        P(),
        P(),
        P(),
        P(),
        P("dp", None),
        P("dp"),
        P("dp", None),
    )
    return jax.shard_map(
        per_device,
        mesh=mesh,
        in_specs=placed,
        out_specs=(
            P("dp", None),
            P("dp", None),
            P(None, "tensor"),
            P("tensor", None),
            P("tensor", None),
            P(),
            P(None, "tensor"),
            P("tensor"),
            P("tensor", None),
            P(),
            P(),
            P(),
            P(),
            P(),
        ),
        check_vma=False,
    )
```
